32 devices in a mesh: file: 2 (over x), seq: 4 (over z), tp: 4 (over y, core).
Axes of the slice: x: 2, y: 2, z: 4, core: 2. Of those that a mesh axis runs over, the one named last changes fastest.
Arguments:
- queries: bfloat16 [4096, 4096], P(('file', 'tp', 'seq')), parts along dimension 0
- keys: bfloat16 [4096, 1024], P(('file', 'tp', 'seq')), parts along dimension 0
- values: bfloat16 [4096, 1024], P(('file', 'tp', 'seq')), parts along dimension 0, may hold values from -6 to 6
- mem_pos: int32 [256], P(('file', 'tp', 'seq')), parts along dimension 0, may hold values from 0 to 2047, as said below
- norm_gain: float32 [4096], replicated, may hold values from 0.1 to 1.9
- summary_weight: bfloat16 [4096, 6144], P('tp', 'seq'), may hold values from -0.09375 to 0.09375
Outputs:
- encoded: bfloat16 [4096, 4096], P(('file', 'tp', 'seq')), parts along dimension 0
- summary: bfloat16 [256, 6144], P(('file', 'tp'), 'seq'), parts along dimension 0
The draws below stay inside these ranges and needn't reach their ends.
There are 2 independent parts, one for each index of `file`. The reference program is written for one: setup_inputs(seed, part) draws one part's arguments, and reference() takes and returns one part's arrays. A program takes and returns all parts, laid end to end along the dimension named above; an argument that names none is the same for every part. Nothing has to cross between parts.
Inputs may be any that keep to these rules, and one draw needn't show every extreme that they name: `mem_pos`: entry j lies among rows 16 * j to 16 * j + 15.
All inputs are finite; a program needn't handle non-finite values.
Results may differ from the reference program's by a relative error of at most 0.018.
Values may be sent and summed in bfloat16 or wider, within the bound.
A program may use at most 64 MiB of HBM per device.

```python
import jax
import jax.numpy as jnp
from jax import lax

D = 4096
HEADS = 32
KV_HEADS = 8
HEAD_DIM = 128
GROUP = 16
SEQ_LEN = 2048
WINDOW = 512
MEM = 128
QKV_OUT = 6144


def draw_queries(key, part):
    key = jax.random.fold_in(key, 11)
    base = jnp.clip(jax.random.normal(key, (SEQ_LEN, HEADS, HEAD_DIM), jnp.float32), -4.0, 4.0)
    return base.reshape(SEQ_LEN, HEADS * HEAD_DIM).astype(jnp.bfloat16)


def draw_keys(key, part):
    key = jax.random.fold_in(key, 23)
    base = jnp.clip(jax.random.normal(key, (SEQ_LEN, KV_HEADS, HEAD_DIM), jnp.float32), -4.0, 4.0)
    return base.reshape(SEQ_LEN, KV_HEADS * HEAD_DIM).astype(jnp.bfloat16)


def draw_mem_pos(key, part):
    key = jax.random.fold_in(key, 5)
    offsets = jax.random.randint(key, (MEM,), 0, GROUP, dtype=jnp.int32)
    index = jnp.arange(MEM, dtype=jnp.int32)
    offsets = jnp.where(index == 0, 0, offsets)
    offsets = jnp.where(index == MEM - 1, GROUP - 1, offsets)
    return offsets + GROUP * index


def shard_levels(key, extent, cuts, low, top_value):
    level, own = 1.0, jax.random.fold_in(key, 6)
    for position, blocks in cuts:
        steps = jnp.exp(jax.random.uniform(jax.random.fold_in(own, position), (blocks,), jnp.float32, low / len(cuts), top_value / len(cuts)))
        level = level * jnp.repeat(steps, extent[position] // blocks).reshape([-1 if axis == position else 1 for axis in range(len(extent))])
    return level


def scatter_about(key, dims, scale, most, pieces=(), held_as=jnp.bfloat16):
    factor_of = shard_levels(key, dims, pieces, -0.22, 0.18) if pieces else 1.0
    result = jax.random.normal(key, dims, jnp.float32) * scale * factor_of
    return jnp.minimum(jnp.maximum(result, -most), most).astype(held_as)


def setup_inputs(seed: int = 0, part: int = 0) -> dict:
    streams_of = jax.random.split(jax.random.key(seed), 7)
    part_splits = jax.random.split(jax.random.fold_in(streams_of[6], part), 7)
    queries = draw_queries(jax.random.fold_in(jax.random.fold_in(streams_of[6], part), 71), part)
    keys = draw_keys(jax.random.fold_in(jax.random.fold_in(streams_of[6], part), 71), part)
    values = scatter_about(part_splits[2], (SEQ_LEN, KV_HEADS * HEAD_DIM), 1.0, 6.0, ((0, 16),))
    mem_pos = draw_mem_pos(jax.random.fold_in(jax.random.fold_in(streams_of[6], part), 71), part)
    norm_gain = jnp.clip(1.0 + 0.18 * jax.random.normal(streams_of[4], (D,), jnp.float32), 0.1, 1.9)
    summary_weight = scatter_about(streams_of[5], (D, QKV_OUT), D ** -0.5, 0.09375, ((0, 4), (1, 4)))
    return {"queries": queries, "keys": keys, "values": values, "mem_pos": mem_pos, "norm_gain": norm_gain, "summary_weight": summary_weight}


def reference(queries, keys, values, mem_pos, norm_gain, summary_weight):
    group = HEADS // KV_HEADS
    scale = 1.0 / HEAD_DIM ** 0.5
    block = 512 if SEQ_LEN % 512 == 0 else SEQ_LEN
    query_heads = queries.reshape(SEQ_LEN, HEADS, HEAD_DIM)
    key_heads = jnp.pad(keys.reshape(SEQ_LEN, KV_HEADS, HEAD_DIM), ((WINDOW, 0), (0, 0), (0, 0)))
    value_heads = jnp.pad(values.reshape(SEQ_LEN, KV_HEADS, HEAD_DIM), ((WINDOW, 0), (0, 0), (0, 0)))

    def one_head(head):
        kv_index = head // group
        q_head = lax.dynamic_index_in_dim(query_heads, head, 1, keepdims=False)
        k_head = lax.dynamic_index_in_dim(key_heads, kv_index, 1, keepdims=False)
        v_head = lax.dynamic_index_in_dim(value_heads, kv_index, 1, keepdims=False)

        def one_block(index):
            first = (index * block).astype(jnp.int32)
            q_block = lax.dynamic_slice_in_dim(q_head, first, block, 0)
            k_block = lax.dynamic_slice_in_dim(k_head, first, WINDOW + block, 0)
            v_block = lax.dynamic_slice_in_dim(v_head, first, WINDOW + block, 0)
            q_where = first + jnp.arange(block, dtype=jnp.int32)
            k_where = first - WINDOW + jnp.arange(WINDOW + block, dtype=jnp.int32)
            seen = (k_where[None, :] <= q_where[:, None]) & (k_where[None, :] > q_where[:, None] - WINDOW) & (k_where[None, :] >= 0)
            scores = jnp.dot(q_block, k_block.T, preferred_element_type=jnp.float32) * scale
            masked = jnp.where(seen, scores, -jnp.inf)
            peak = lax.optimization_barrier(jnp.max(masked, axis=1, keepdims=True))
            weights = jnp.where(seen, jnp.exp(scores - peak), 0.0)
            total = lax.optimization_barrier(jnp.sum(weights, axis=1, keepdims=True))
            mixed = jnp.dot(weights.astype(jnp.bfloat16), v_block, preferred_element_type=jnp.float32)
            return mixed / total
        parts = lax.map(one_block, jnp.arange(SEQ_LEN // block, dtype=jnp.int32))
        return parts.reshape(SEQ_LEN, HEAD_DIM)
    outputs = lax.map(one_head, jnp.arange(HEADS, dtype=jnp.int32))
    encoded = jnp.transpose(outputs, (1, 0, 2)).reshape(SEQ_LEN, D).astype(jnp.bfloat16)
    picked = jnp.take(encoded, mem_pos.astype(jnp.int32), axis=0).astype(jnp.float32)
    meansq = lax.optimization_barrier(jnp.mean(picked * picked, axis=1, keepdims=True))
    normed = (picked * lax.rsqrt(meansq + 1e-05) * norm_gain[None, :]).astype(jnp.bfloat16)
    summary = jnp.dot(normed, summary_weight, preferred_element_type=jnp.float32).astype(jnp.bfloat16)
    return (encoded, summary)
```

```python
import functools
import math

import jax
import jax.numpy as jnp
from jax import lax
from jax.experimental import pallas as pl
from jax.experimental.pallas import tpu as pltpu
from jax.sharding import PartitionSpec as P

D = 4096
HEADS = 32
KV_HEADS = 8
HEAD_DIM = 128
WINDOW = 512
SHARE = HEADS // KV_HEADS
MESH = pl.DeviceIdType.MESH
AHEAD = 3


def kernel(
    n_tp, n_seq, prior,
    q_hbm, k_ref, v_ref, pos_ref, gain_ref, w_hbm,
    enc_ref, sum_ref,
    q_buf, w_buf, kv, bias, picked, mine, mem, part, red,
    local_sem, kv_send, kv_recv, mem_send, mem_recv, red_send, red_recv,
):
    tp = lax.axis_index("tp")
    seq = lax.axis_index("seq")
    me = tp * n_seq + seq
    n = n_tp * n_seq
    rows = k_ref.shape[0]
    span = (prior + 1) * rows
    picks = pos_ref.shape[0]
    width = D // n_tp
    half = width // 2
    cols = sum_ref.shape[1]
    tile = 512 if cols % 512 == 0 else cols

    def device(index):
        return {"tp": index // n_seq, "seq": index % n_seq}

    q_copy = pltpu.make_async_copy(q_hbm, q_buf, local_sem.at[0])
    w_copy = pltpu.make_async_copy(w_hbm, w_buf, local_sem.at[1])
    q_copy.start()
    w_copy.start()

    barrier = pltpu.get_barrier_semaphore()

    @pl.loop(1, n)
    def _(step):
        pl.semaphore_signal(
            barrier, inc=1, device_id=device((me + step) % n), device_id_type=MESH
        )

    for g in range(KV_HEADS):
        kv[g, 0, prior * rows :, :] = k_ref[:, g * HEAD_DIM : (g + 1) * HEAD_DIM]
        kv[g, 1, prior * rows :, :] = v_ref[:, g * HEAD_DIM : (g + 1) * HEAD_DIM]
    for k in range(1, prior + 1):

        @pl.when(me < k)
        def _():
            start = (prior - k) * rows
            kv[:, :, start : start + rows, :] = jnp.zeros(
                (KV_HEADS, 2, rows, HEAD_DIM), jnp.bfloat16
            )

    row = lax.broadcasted_iota(jnp.int32, (rows, span), 0)
    col = lax.broadcasted_iota(jnp.int32, (rows, span), 1) - prior * rows
    seen = (col <= row) & (col > row - WINDOW) & (col + me * rows >= 0)
    bias[...] = jnp.where(seen, 0.0, -jnp.inf).astype(jnp.float32)

    pick_row = lax.broadcasted_iota(jnp.int32, (picks, rows), 0)
    pick_col = lax.broadcasted_iota(jnp.int32, (picks, rows), 1)
    wanted = jnp.zeros((picks, rows), jnp.int32)
    for j in range(picks):
        wanted = jnp.where(pick_row == j, pos_ref[j] - me * rows, wanted)
    choose = jnp.where(pick_col == wanted, 1.0, 0.0).astype(jnp.bfloat16)

    def slot(c, k):
        return kv.at[c, :, pl.ds((prior - k) * rows, rows), :]

    def send(c, k, lands, way, target):
        return pltpu.make_async_remote_copy(
            src_ref=slot(c, k),
            dst_ref=slot(c, lands),
            send_sem=kv_send.at[way, k, c],
            recv_sem=kv_recv.at[lands, c],
            device_id=target,
            device_id_type=MESH,
        )

    def up(c, k):
        return send(c, k, k + 1, 0, {"tp": tp, "seq": seq + 1})

    def down(c, k):
        return send(c, k, k - 1, 1, {"tp": tp, "seq": seq - 1})

    def far(c):
        return send(c, 0, prior, 1, {"tp": tp + 1, "seq": seq + prior - n_seq})

    has_up = seq + 1 < n_seq
    has_far = (seq + prior >= n_seq) & (tp + 1 < n_tp)

    def own(c):
        @pl.when(has_up)
        def _():
            up(c, 0).start()

        @pl.when(has_far)
        def _():
            far(c).start()

    def from_below(c, k):
        @pl.when(seq >= k)
        def _():
            up(c, k - 1).wait_recv()

            if k < prior:

                @pl.when(has_up)
                def _():
                    up(c, k).start()

    def from_before(c, k):
        @pl.when((seq < k) & (tp > 0))
        def _():
            send(c, 0, k, 1, {"tp": tp, "seq": seq}).wait_recv()

            if k >= 2:

                @pl.when(seq >= 1)
                def _():
                    down(c, k).start()

    fold = math.log2(math.e) / HEAD_DIM**0.5

    def attend(g):
        first = pl.multiple_of(g * SHARE * HEAD_DIM, SHARE * HEAD_DIM)
        q_all = q_buf[:, pl.ds(first, SHARE * HEAD_DIM)]
        q_rows = jnp.concatenate(
            [q_all[:, h * HEAD_DIM : (h + 1) * HEAD_DIM] for h in range(SHARE)], axis=0
        )
        scores = lax.dot_general(
            q_rows, kv[g, 0], (((1,), (1,)), ((), ())), preferred_element_type=jnp.float32
        )
        values = kv[g, 1]
        outs = []
        for h in range(SHARE):
            masked = scores[h * rows : (h + 1) * rows] + bias[...]
            peak = jnp.max(masked, axis=1, keepdims=True)
            weights = jnp.exp2((masked - peak) * fold)
            total = jnp.sum(weights, axis=1, keepdims=True)
            mixed = jnp.dot(
                weights.astype(jnp.bfloat16), values, preferred_element_type=jnp.float32
            )
            outs.append((mixed / total).astype(jnp.bfloat16))
        encoded = jnp.concatenate(outs, axis=1)
        enc_ref[:, pl.ds(first, SHARE * HEAD_DIM)] = encoded
        picked[:, pl.ds(first, SHARE * HEAD_DIM)] = jnp.dot(
            choose, encoded, preferred_element_type=jnp.float32
        )

    pl.semaphore_wait(barrier, n - 1)
    for c in range(AHEAD):
        own(c)
    q_copy.wait()

    @pl.loop(0, KV_HEADS + prior - 1)
    def _(t):
        @pl.when(t + AHEAD < KV_HEADS)
        def _():
            own(t + AHEAD)

        for depth in range(1, prior + 1):
            c = t - (depth - 1)

            @pl.when((c >= 0) & (c < KV_HEADS))
            def _():
                from_below(c, depth)
                from_before(c, prior + 1 - depth)

        @pl.when(t >= prior - 1)
        def _():
            attend(t - (prior - 1))

    x = picked[...]
    meansq = jnp.mean(x * x, axis=1, keepdims=True)
    normed = x * lax.rsqrt(meansq + 1e-05) * gain_ref[...]
    for t in range(n_tp):
        left = normed[:, t * width : t * width + half]
        right = normed[:, t * width + half : (t + 1) * width]
        mine[t] = jnp.concatenate((left, right), axis=0).astype(jnp.bfloat16)

    def share(step):
        other = (me + step) % n
        return pltpu.make_async_remote_copy(
            src_ref=mine.at[other // n_seq],
            dst_ref=mem.at[me],
            send_sem=mem_send.at[step],
            recv_sem=mem_recv.at[me],
            device_id=device(other),
            device_id_type=MESH,
        )

    @pl.loop(1, n)
    def _(step):
        share(step).start()

    mem[me] = mine[tp]
    w_copy.wait()

    @pl.loop(1, n)
    def _(step):
        source = (me + step) % n
        pltpu.make_async_remote_copy(
            src_ref=mine.at[0],
            dst_ref=mem.at[source],
            send_sem=mem_send.at[step],
            recv_sem=mem_recv.at[source],
            device_id=device(source),
            device_id_type=MESH,
        ).wait_recv()

    gathered = mem[...].astype(jnp.float32)
    left = gathered[:, :picks].reshape(n * picks, half)
    right = gathered[:, picks:].reshape(n * picks, half)
    memory = jnp.concatenate((left, right), axis=1).astype(jnp.bfloat16)

    def reduce(step, j):
        other = (tp + step) % n_tp
        return pltpu.make_async_remote_copy(
            src_ref=part.at[other, :, pl.ds(j * tile, tile)],
            dst_ref=red.at[tp, :, pl.ds(j * tile, tile)],
            send_sem=red_send.at[step, j],
            recv_sem=red_recv.at[tp, j],
            device_id={"tp": other, "seq": seq},
            device_id_type=MESH,
        )

    for j in range(cols // tile):
        sums = jnp.dot(
            memory, w_buf[:, j * tile : (j + 1) * tile], preferred_element_type=jnp.float32
        )
        part[:, :, j * tile : (j + 1) * tile] = sums.reshape(n_tp, n_seq * picks, tile).astype(
            jnp.bfloat16
        )
        for step in range(1, n_tp):
            reduce(step, j).start()

    for j in range(cols // tile):
        where = slice(j * tile, (j + 1) * tile)
        total = part[tp, :, where].astype(jnp.float32)
        for step in range(1, n_tp):
            source = (tp + step) % n_tp
            pltpu.make_async_remote_copy(
                src_ref=part.at[0, :, pl.ds(j * tile, tile)],
                dst_ref=red.at[source, :, pl.ds(j * tile, tile)],
                send_sem=red_send.at[step, j],
                recv_sem=red_recv.at[source, j],
                device_id={"tp": source, "seq": seq},
                device_id_type=MESH,
            ).wait_recv()
            total = total + red[source, :, where].astype(jnp.float32)
        sum_ref[:, where] = total.astype(jnp.bfloat16)

    for j in range(cols // tile):
        for step in range(1, n_tp):
            reduce(step, j).wait_send()

    @pl.loop(1, n)
    def _(step):
        share(step).wait_send()

    @pl.loop(0, KV_HEADS)
    def _(c):
        @pl.when(has_up)
        def _():
            up(c, 0).wait_send()

        @pl.when(has_far)
        def _():
            far(c).wait_send()

        for k in range(1, prior):

            @pl.when((seq >= k) & has_up)
            def _():
                up(c, k).wait_send()

        for k in range(2, prior + 1):

            @pl.when((seq < k) & (tp > 0) & (seq >= 1))
            def _():
                down(c, k).wait_send()


def on_device(n_tp, n_seq, queries, keys, values, mem_pos, norm_gain, summary_weight):
    rows = queries.shape[0]
    picks = mem_pos.shape[0]
    prior = -(-(WINDOW - 1) // rows)
    n = n_tp * n_seq
    width = summary_weight.shape[0]
    cols = summary_weight.shape[1]
    tiles = cols // 512 if cols % 512 == 0 else 1
    vmem = pl.BlockSpec(memory_space=pltpu.VMEM)
    anywhere = pl.BlockSpec(memory_space=pl.ANY)
    bf16 = jnp.bfloat16
    dma = pltpu.SemaphoreType.DMA
    span = (prior + 1) * rows
    return pl.pallas_call(
        functools.partial(kernel, n_tp, n_seq, prior),
        out_shape=(
            jax.ShapeDtypeStruct((rows, D), bf16),
            jax.ShapeDtypeStruct((n_seq * picks, cols), bf16),
        ),
        in_specs=[
            anywhere, vmem, vmem, pl.BlockSpec(memory_space=pltpu.SMEM), vmem, anywhere,
        ],
        out_specs=(vmem, vmem),
        scratch_shapes=[
            pltpu.VMEM((rows, D), bf16),
            pltpu.VMEM((width, cols), bf16),
            pltpu.VMEM((KV_HEADS, 2, span, HEAD_DIM), bf16),
            pltpu.VMEM((rows, span), jnp.float32),
            pltpu.VMEM((picks, D), jnp.float32),
            pltpu.VMEM((n_tp, 2 * picks, width // 2), bf16),
            pltpu.VMEM((n, 2 * picks, width // 2), bf16),
            pltpu.VMEM((n_tp, n_seq * picks, cols), bf16),
            pltpu.VMEM((n_tp, n_seq * picks, cols), bf16),
            dma((2,)),
            dma((2, prior + 1, KV_HEADS)),
            dma((prior + 1, KV_HEADS)),
            dma((n,)),
            dma((n,)),
            dma((n_tp, tiles)),
            dma((n_tp, tiles)),
        ],
        compiler_params=pltpu.CompilerParams(
            collective_id=0, has_side_effects=True, vmem_limit_bytes=60 * 1024 * 1024
        ),
        cost_estimate=pl.CostEstimate(
            flops=4 * HEADS * rows * span * HEAD_DIM + 2 * n * picks * width * cols,
            bytes_accessed=2 * (2 * rows * D + 4 * rows * KV_HEADS * HEAD_DIM + width * cols),
            transcendentals=HEADS * rows * span,
        ),
    )(queries, keys, values, mem_pos, norm_gain.reshape(1, D), summary_weight)


def solution(mesh):
    placed = (
        P(("file", "tp", "seq"), None),
        P(("file", "tp", "seq"), None),
        P(("file", "tp", "seq"), None),
        P(("file", "tp", "seq")),
        P(),
        P("tp", "seq"),
    )
    return jax.shard_map(
        functools.partial(on_device, mesh.shape["tp"], mesh.shape["seq"]),
        mesh=mesh,
        in_specs=placed,
        out_specs=(P(("file", "tp", "seq"), None), P(("file", "tp"), "seq")),
        check_vma=False,
    )
```

```python
import functools
import math

import jax
import jax.numpy as jnp
from jax import lax
from jax.experimental import pallas as pl
from jax.experimental.pallas import tpu as pltpu
from jax.sharding import PartitionSpec as P

D = 4096
HEADS = 32
KV_HEADS = 8
HEAD_DIM = 128
WINDOW = 512
SHARE = HEADS // KV_HEADS
MESH = pl.DeviceIdType.MESH
AHEAD = 3
PIECES = 4


def hand_over(enc_from, sum_from, enc_to, sum_to, sems):
    rows = enc_from.shape[0] // PIECES
    copies = [pltpu.make_async_copy(sum_from, sum_to, sems.at[PIECES])]
    for i in range(PIECES):
        piece = pl.ds(i * rows, rows)
        copies.append(pltpu.make_async_copy(enc_from.at[piece], enc_to.at[piece], sems.at[i]))
    for copy in copies:
        copy.start()
    for copy in copies:
        copy.wait()


def kernel(
    n_tp, n_seq, prior,
    q_hbm, k_ref, v_ref, pos_ref, gain_ref, w_hbm,
    enc_ref, sum_ref,
    q_buf, w_buf, kv, bias, squares, mine, mem, sums, part, red, scales,
    local_sem, kv_send, kv_recv, mem_send, mem_recv, red_send, red_recv, scale_send, scale_recv,
):
    tp = lax.axis_index("tp")
    seq = lax.axis_index("seq")
    me = tp * n_seq + seq
    n = n_tp * n_seq
    rows = k_ref.shape[0]
    span = (prior + 1) * rows
    picks = pos_ref.shape[0]
    per = KV_HEADS // n_tp
    columns = SHARE * HEAD_DIM
    half = columns // 2
    cols = sum_ref.shape[1]
    tile = 512 if cols % 512 == 0 else cols
    squares[...] = jnp.zeros_like(squares)
    sums[...] = jnp.zeros_like(sums)

    def device(index):
        return {"tp": index // n_seq, "seq": index % n_seq}

    q_copy = pltpu.make_async_copy(q_hbm, q_buf, local_sem.at[0])
    w_copy = pltpu.make_async_copy(w_hbm, w_buf, local_sem.at[1])
    q_copy.start()
    w_copy.start()

    barrier = pltpu.get_barrier_semaphore()

    @pl.loop(1, n)
    def _(step):
        pl.semaphore_signal(
            barrier, inc=1, device_id=device((me + step) % n), device_id_type=MESH
        )

    for g in range(KV_HEADS):
        kv[g, 0, prior * rows :, :] = k_ref[:, g * HEAD_DIM : (g + 1) * HEAD_DIM]
        kv[g, 1, prior * rows :, :] = v_ref[:, g * HEAD_DIM : (g + 1) * HEAD_DIM]
    for k in range(1, prior + 1):

        @pl.when(me < k)
        def _():
            start = (prior - k) * rows
            kv[:, :, start : start + rows, :] = jnp.zeros(
                (KV_HEADS, 2, rows, HEAD_DIM), jnp.bfloat16
            )

    row = lax.broadcasted_iota(jnp.int32, (rows, span), 0)
    col = lax.broadcasted_iota(jnp.int32, (rows, span), 1) - prior * rows
    seen = (col <= row) & (col > row - WINDOW) & (col + me * rows >= 0)
    bias[...] = jnp.where(seen, 0.0, -jnp.inf).astype(jnp.float32)

    pick_row = lax.broadcasted_iota(jnp.int32, (picks, rows), 0)
    pick_col = lax.broadcasted_iota(jnp.int32, (picks, rows), 1)
    wanted = jnp.zeros((picks, rows), jnp.int32)
    for j in range(picks):
        wanted = jnp.where(pick_row == j, pos_ref[j] - me * rows, wanted)
    choose = jnp.where(pick_col == wanted, 1.0, 0.0).astype(jnp.bfloat16)

    def slot(c, k):
        return kv.at[c, :, pl.ds((prior - k) * rows, rows), :]

    def send(c, k, lands, way, target):
        return pltpu.make_async_remote_copy(
            src_ref=slot(c, k),
            dst_ref=slot(c, lands),
            send_sem=kv_send.at[way, k, c],
            recv_sem=kv_recv.at[lands, c],
            device_id=target,
            device_id_type=MESH,
        )

    def up(c, k):
        return send(c, k, k + 1, 0, {"tp": tp, "seq": seq + 1})

    def down(c, k):
        return send(c, k, k - 1, 1, {"tp": tp, "seq": seq - 1})

    def far(c):
        return send(c, 0, prior, 1, {"tp": tp + 1, "seq": seq + prior - n_seq})

    has_up = seq + 1 < n_seq
    has_far = (seq + prior >= n_seq) & (tp + 1 < n_tp)

    def own(c):
        @pl.when(has_up)
        def _():
            up(c, 0).start()

        @pl.when(has_far)
        def _():
            far(c).start()

    def from_below(c, k):
        @pl.when(seq >= k)
        def _():
            up(c, k - 1).wait_recv()

            if k < prior:

                @pl.when(has_up)
                def _():
                    up(c, k).start()

    def from_before(c, k):
        @pl.when((seq < k) & (tp > 0))
        def _():
            send(c, 0, k, 1, {"tp": tp, "seq": seq}).wait_recv()

            if k >= 2:

                @pl.when(seq >= 1)
                def _():
                    down(c, k).start()

    fold = math.log2(math.e) / HEAD_DIM**0.5

    def attend(g):
        first = pl.multiple_of(g * SHARE * HEAD_DIM, SHARE * HEAD_DIM)
        q_all = q_buf[:, pl.ds(first, SHARE * HEAD_DIM)]
        q_rows = jnp.concatenate(
            [q_all[:, h * HEAD_DIM : (h + 1) * HEAD_DIM] for h in range(SHARE)], axis=0
        )
        scores = lax.dot_general(
            q_rows, kv[g, 0], (((1,), (1,)), ((), ())), preferred_element_type=jnp.float32
        )
        values = kv[g, 1]
        outs = []
        for h in range(SHARE):
            masked = scores[h * rows : (h + 1) * rows] + bias[...]
            peak = jnp.max(masked, axis=1, keepdims=True)
            weights = jnp.exp2((masked - peak) * fold)
            total = jnp.sum(weights, axis=1, keepdims=True)
            mixed = jnp.dot(
                weights.astype(jnp.bfloat16), values, preferred_element_type=jnp.float32
            )
            outs.append((mixed / total).astype(jnp.bfloat16))
        encoded = jnp.concatenate(outs, axis=1)
        enc_ref[:, pl.ds(first, SHARE * HEAD_DIM)] = encoded
        picked = jnp.dot(choose, encoded, preferred_element_type=jnp.float32)
        squared = picked * picked
        for h in range(SHARE):
            squares[...] += squared[:, h * HEAD_DIM : (h + 1) * HEAD_DIM]
        gained = picked * gain_ref[:, pl.ds(first, columns)]
        mine[g] = jnp.concatenate((gained[:, :half], gained[:, half:]), axis=0).astype(jnp.bfloat16)

    def share(g, s, source):
        return pltpu.make_async_remote_copy(
            src_ref=mine.at[g],
            dst_ref=mem.at[g % per, source],
            send_sem=mem_send.at[g, s],
            recv_sem=mem_recv.at[g % per, source],
            device_id={"tp": g // per, "seq": s},
            device_id_type=MESH,
        )

    def each_share(g, act):
        for step in range(1, n_seq):
            act(share(g, (seq + step) % n_seq, me))

        @pl.when(g // per != tp)
        def _():
            act(share(g, seq, me))

    def scale_to(step):
        return pltpu.make_async_remote_copy(
            src_ref=scales.at[seq],
            dst_ref=scales.at[seq],
            send_sem=scale_send.at[step],
            recv_sem=scale_recv.at[seq],
            device_id={"tp": tp, "seq": (seq + step) % n_seq},
            device_id_type=MESH,
        )

    def reduce(step):
        other = (tp + step) % n_tp
        return pltpu.make_async_remote_copy(
            src_ref=part.at[other],
            dst_ref=red.at[tp],
            send_sem=red_send.at[step],
            recv_sem=red_recv.at[tp],
            device_id={"tp": other, "seq": seq},
            device_id_type=MESH,
        )

    def project(g):
        place = g % per

        @pl.loop(1, n)
        def _(step):
            source = (me + step) % n
            share(per * tp + place, seq, source).wait_recv()

        gathered = mem[place].astype(jnp.float32)
        left = gathered[:, :picks].reshape(n * picks, half)
        right = gathered[:, picks:].reshape(n * picks, half)
        memory = jnp.concatenate((left, right), axis=1).astype(jnp.bfloat16)
        down_to = pl.multiple_of(place * columns, columns)
        for j in range(cols // tile):
            where = slice(j * tile, (j + 1) * tile)
            sums[:, where] += jnp.dot(
                memory, w_buf[pl.ds(down_to, columns), where], preferred_element_type=jnp.float32
            )

        @pl.when(place == per - 1)
        def _():
            part[...] = sums[...].reshape(n_tp, n_seq * picks, cols).astype(jnp.bfloat16)
            for step in range(1, n_tp):
                reduce(step).start()

    pl.semaphore_wait(barrier, n - 1)
    for c in range(AHEAD):
        own(c)
    q_copy.wait()
    w_copy.wait()

    @pl.loop(0, KV_HEADS + prior)
    def _(t):
        @pl.when(t + AHEAD < KV_HEADS)
        def _():
            own(t + AHEAD)

        for depth in range(1, prior + 1):
            c = t - (depth - 1)

            @pl.when((c >= 0) & (c < KV_HEADS))
            def _():
                from_below(c, depth)
                from_before(c, prior + 1 - depth)

        g = t - (prior - 1)

        @pl.when((g >= 0) & (g < KV_HEADS))
        def _():
            attend(g)
            each_share(g, lambda copy: copy.start())

            @pl.when(g // per == tp)
            def _():
                mem[g % per, me] = mine[g]

        @pl.when(g == KV_HEADS - 1)
        def _():
            meansq = jnp.sum(squares[...], axis=1, keepdims=True) / D
            scales[seq] = jnp.broadcast_to(lax.rsqrt(meansq + 1e-05), scales.shape[1:])
            for step in range(1, n_seq):
                scale_to(step).start()

        @pl.when((g >= 1) & ((g - 1) // per == tp))
        def _():
            project(g - 1)

    total = part[tp].astype(jnp.float32)
    for step in range(1, n_tp):
        source = (tp + step) % n_tp
        pltpu.make_async_remote_copy(
            src_ref=part.at[0],
            dst_ref=red.at[source],
            send_sem=red_send.at[step],
            recv_sem=red_recv.at[source],
            device_id={"tp": source, "seq": seq},
            device_id_type=MESH,
        ).wait_recv()
        total = total + red[source].astype(jnp.float32)
    for step in range(1, n_seq):
        source = (seq + step) % n_seq
        pltpu.make_async_remote_copy(
            src_ref=scales.at[source],
            dst_ref=scales.at[source],
            send_sem=scale_send.at[step],
            recv_sem=scale_recv.at[source],
            device_id={"tp": tp, "seq": source},
            device_id_type=MESH,
        ).wait_recv()
    factor = scales[...].reshape(n_seq * picks, HEAD_DIM)[:, :1]
    sum_ref[...] = (total * factor).astype(jnp.bfloat16)

    for step in range(1, n_tp):
        reduce(step).wait_send()
    for step in range(1, n_seq):
        scale_to(step).wait_send()

    @pl.loop(0, KV_HEADS)
    def _(g):
        each_share(g, lambda copy: copy.wait_send())

    @pl.loop(0, KV_HEADS)
    def _(c):
        @pl.when(has_up)
        def _():
            up(c, 0).wait_send()

        @pl.when(has_far)
        def _():
            far(c).wait_send()

        for k in range(1, prior):

            @pl.when((seq >= k) & has_up)
            def _():
                up(c, k).wait_send()

        for k in range(2, prior + 1):

            @pl.when((seq < k) & (tp > 0) & (seq >= 1))
            def _():
                down(c, k).wait_send()


def on_device(n_tp, n_seq, queries, keys, values, mem_pos, norm_gain, summary_weight):
    rows = queries.shape[0]
    picks = mem_pos.shape[0]
    prior = -(-(WINDOW - 1) // rows)
    n = n_tp * n_seq
    width = summary_weight.shape[0]
    cols = summary_weight.shape[1]
    per = KV_HEADS // n_tp
    half = width // per // 2
    vmem = pl.BlockSpec(memory_space=pltpu.VMEM)
    anywhere = pl.BlockSpec(memory_space=pl.ANY)
    bf16 = jnp.bfloat16
    dma = pltpu.SemaphoreType.DMA
    span = (prior + 1) * rows
    results = pl.pallas_call(
        functools.partial(kernel, n_tp, n_seq, prior),
        out_shape=(
            jax.ShapeDtypeStruct((rows, D), bf16),
            jax.ShapeDtypeStruct((n_seq * picks, cols), bf16),
        ),
        in_specs=[
            anywhere, vmem, vmem, pl.BlockSpec(memory_space=pltpu.SMEM), vmem, anywhere,
        ],
        out_specs=(vmem, vmem),
        scratch_shapes=[
            pltpu.VMEM((rows, D), bf16),
            pltpu.VMEM((width, cols), bf16),
            pltpu.VMEM((KV_HEADS, 2, span, HEAD_DIM), bf16),
            pltpu.VMEM((rows, span), jnp.float32),
            pltpu.VMEM((picks, HEAD_DIM), jnp.float32),
            pltpu.VMEM((KV_HEADS, 2 * picks, half), bf16),
            pltpu.VMEM((per, n, 2 * picks, half), bf16),
            pltpu.VMEM((n * picks, cols), jnp.float32),
            pltpu.VMEM((n_tp, n_seq * picks, cols), bf16),
            pltpu.VMEM((n_tp, n_seq * picks, cols), bf16),
            pltpu.VMEM((n_seq, picks, HEAD_DIM), jnp.float32),
            dma((2,)),
            dma((2, prior + 1, KV_HEADS)),
            dma((prior + 1, KV_HEADS)),
            dma((KV_HEADS, n_seq)),
            dma((per, n)),
            dma((n_tp,)),
            dma((n_tp,)),
            dma((n_seq,)),
            dma((n_seq,)),
        ],
        compiler_params=pltpu.CompilerParams(
            collective_id=0, has_side_effects=True, vmem_limit_bytes=60 * 1024 * 1024
        ),
        cost_estimate=pl.CostEstimate(
            flops=4 * HEADS * rows * span * HEAD_DIM + 2 * n * picks * width * cols,
            bytes_accessed=2 * (2 * rows * D + 4 * rows * KV_HEADS * HEAD_DIM + width * cols),
            transcendentals=HEADS * rows * span,
        ),
    )(queries, keys, values, mem_pos, norm_gain.reshape(1, D), summary_weight)
    return pl.pallas_call(
        hand_over,
        out_shape=tuple(jax.ShapeDtypeStruct(r.shape, r.dtype) for r in results),
        in_specs=[anywhere, anywhere],
        out_specs=(anywhere, anywhere),
        scratch_shapes=[dma((PIECES + 1,))],
        compiler_params=pltpu.CompilerParams(vmem_limit_bytes=60 * 1024 * 1024),
    )(*results)


def solution(mesh):
    placed = (
        P(("file", "tp", "seq"), None),
        P(("file", "tp", "seq"), None),
        P(("file", "tp", "seq"), None),
        P(("file", "tp", "seq")),
        P(),
        P("tp", "seq"),
    )
    return jax.shard_map(
        functools.partial(on_device, mesh.shape["tp"], mesh.shape["seq"]),
        mesh=mesh,
        in_specs=placed,
        out_specs=(P(("file", "tp", "seq"), None), P(("file", "tp"), "seq")),
        check_vma=False,
    )
```

```python
import functools
import math

import jax
import jax.numpy as jnp
from jax import lax
from jax.experimental import pallas as pl
from jax.experimental.pallas import tpu as pltpu
from jax.sharding import PartitionSpec as P

D = 4096
HEADS = 32
KV_HEADS = 8
HEAD_DIM = 128
WINDOW = 512
SHARE = HEADS // KV_HEADS
MESH = pl.DeviceIdType.MESH
AHEAD = 3
PIECES = 4


def hand_over(enc_from, sum_from, enc_to, sum_to, enc_buf, sum_buf, sems):
    rows = enc_from.shape[0] // PIECES
    parts = [(sum_from, sum_buf, sum_to)]
    for i in range(PIECES):
        piece = pl.ds(i * rows, rows)
        parts.append((enc_from.at[piece], enc_buf.at[piece], enc_to.at[piece]))
    into = [pltpu.make_async_copy(a, b, sems.at[0, i]) for i, (a, b, c) in enumerate(parts)]
    out = [pltpu.make_async_copy(b, c, sems.at[1, i]) for i, (a, b, c) in enumerate(parts)]
    for copy in into:
        copy.start()
    for first, second in zip(into, out):
        first.wait()
        second.start()
    for copy in out:
        copy.wait()


def kernel(
    n_tp, n_seq, prior,
    q_hbm, k_ref, v_ref, pos_ref, gain_ref, w_hbm,
    enc_ref, sum_ref,
    q_buf, w_buf, kv, bias, squares, mine, mem, sums, part, red, scales,
    local_sem, kv_send, kv_recv, mem_send, mem_recv, red_send, red_recv, scale_send, scale_recv,
):
    tp = lax.axis_index("tp")
    seq = lax.axis_index("seq")
    me = tp * n_seq + seq
    n = n_tp * n_seq
    rows = k_ref.shape[0]
    span = (prior + 1) * rows
    picks = pos_ref.shape[0]
    per = KV_HEADS // n_tp
    columns = SHARE * HEAD_DIM
    half = columns // 2
    cols = sum_ref.shape[1]
    tile = 512 if cols % 512 == 0 else cols
    squares[...] = jnp.zeros_like(squares)
    sums[...] = jnp.zeros_like(sums)

    def device(index):
        return {"tp": index // n_seq, "seq": index % n_seq}

    q_copy = pltpu.make_async_copy(q_hbm, q_buf, local_sem.at[0])
    w_copy = pltpu.make_async_copy(w_hbm, w_buf, local_sem.at[1])
    q_copy.start()
    w_copy.start()

    barrier = pltpu.get_barrier_semaphore()

    @pl.loop(1, n)
    def _(step):
        pl.semaphore_signal(
            barrier, inc=1, device_id=device((me + step) % n), device_id_type=MESH
        )

    for g in range(KV_HEADS):
        kv[g, 0, prior * rows :, :] = k_ref[:, g * HEAD_DIM : (g + 1) * HEAD_DIM]
        kv[g, 1, prior * rows :, :] = v_ref[:, g * HEAD_DIM : (g + 1) * HEAD_DIM]
    for k in range(1, prior + 1):

        @pl.when(me < k)
        def _():
            start = (prior - k) * rows
            kv[:, :, start : start + rows, :] = jnp.zeros(
                (KV_HEADS, 2, rows, HEAD_DIM), jnp.bfloat16
            )

    row = lax.broadcasted_iota(jnp.int32, (rows, span), 0)
    col = lax.broadcasted_iota(jnp.int32, (rows, span), 1) - prior * rows
    seen = (col <= row) & (col > row - WINDOW) & (col + me * rows >= 0)
    bias[...] = jnp.where(seen, 0.0, -jnp.inf).astype(jnp.float32)

    pick_row = lax.broadcasted_iota(jnp.int32, (picks, rows), 0)
    pick_col = lax.broadcasted_iota(jnp.int32, (picks, rows), 1)
    wanted = jnp.zeros((picks, rows), jnp.int32)
    for j in range(picks):
        wanted = jnp.where(pick_row == j, pos_ref[j] - me * rows, wanted)
    choose = jnp.where(pick_col == wanted, 1.0, 0.0).astype(jnp.bfloat16)

    def slot(c, k):
        return kv.at[c, :, pl.ds((prior - k) * rows, rows), :]

    def send(c, k, lands, way, target):
        return pltpu.make_async_remote_copy(
            src_ref=slot(c, k),
            dst_ref=slot(c, lands),
            send_sem=kv_send.at[way, k, c],
            recv_sem=kv_recv.at[lands, c],
            device_id=target,
            device_id_type=MESH,
        )

    def up(c, k):
        return send(c, k, k + 1, 0, {"tp": tp, "seq": seq + 1})

    def down(c, k):
        return send(c, k, k - 1, 1, {"tp": tp, "seq": seq - 1})

    def far(c):
        return send(c, 0, prior, 1, {"tp": tp + 1, "seq": seq + prior - n_seq})

    has_up = seq + 1 < n_seq
    has_far = (seq + prior >= n_seq) & (tp + 1 < n_tp)

    def own(c):
        @pl.when(has_up)
        def _():
            up(c, 0).start()

        @pl.when(has_far)
        def _():
            far(c).start()

    def from_below(c, k):
        @pl.when(seq >= k)
        def _():
            up(c, k - 1).wait_recv()

            if k < prior:

                @pl.when(has_up)
                def _():
                    up(c, k).start()

    def from_before(c, k):
        @pl.when((seq < k) & (tp > 0))
        def _():
            send(c, 0, k, 1, {"tp": tp, "seq": seq}).wait_recv()

            if k >= 2:

                @pl.when(seq >= 1)
                def _():
                    down(c, k).start()

    fold = math.log2(math.e) / HEAD_DIM**0.5

    def attend(g):
        first = pl.multiple_of(g * SHARE * HEAD_DIM, SHARE * HEAD_DIM)
        q_all = q_buf[:, pl.ds(first, SHARE * HEAD_DIM)]
        q_rows = jnp.concatenate(
            [q_all[:, h * HEAD_DIM : (h + 1) * HEAD_DIM] for h in range(SHARE)], axis=0
        )
        scores = lax.dot_general(
            q_rows, kv[g, 0], (((1,), (1,)), ((), ())), preferred_element_type=jnp.float32
        )
        values = kv[g, 1]
        outs = []
        for h in range(SHARE):
            masked = scores[h * rows : (h + 1) * rows] + bias[...]
            peak = jnp.max(masked, axis=1, keepdims=True)
            weights = jnp.exp2((masked - peak) * fold)
            total = jnp.sum(weights, axis=1, keepdims=True)
            mixed = jnp.dot(
                weights.astype(jnp.bfloat16), values, preferred_element_type=jnp.float32
            )
            outs.append((mixed / total).astype(jnp.bfloat16))
        encoded = jnp.concatenate(outs, axis=1)
        enc_ref[:, pl.ds(first, SHARE * HEAD_DIM)] = encoded
        picked = jnp.dot(choose, encoded, preferred_element_type=jnp.float32)
        squared = picked * picked
        for h in range(SHARE):
            squares[...] += squared[:, h * HEAD_DIM : (h + 1) * HEAD_DIM]
        gained = picked * gain_ref[:, pl.ds(first, columns)]
        mine[g] = jnp.concatenate((gained[:, :half], gained[:, half:]), axis=0).astype(jnp.bfloat16)

    def share(g, s, source):
        return pltpu.make_async_remote_copy(
            src_ref=mine.at[g],
            dst_ref=mem.at[g % per, source],
            send_sem=mem_send.at[g, s],
            recv_sem=mem_recv.at[g % per, source],
            device_id={"tp": g // per, "seq": s},
            device_id_type=MESH,
        )

    def each_share(g, act):
        for step in range(1, n_seq):
            act(share(g, (seq + step) % n_seq, me))

        @pl.when(g // per != tp)
        def _():
            act(share(g, seq, me))

    def scale_to(step):
        return pltpu.make_async_remote_copy(
            src_ref=scales.at[seq],
            dst_ref=scales.at[seq],
            send_sem=scale_send.at[step],
            recv_sem=scale_recv.at[seq],
            device_id={"tp": tp, "seq": (seq + step) % n_seq},
            device_id_type=MESH,
        )

    def reduce(step):
        other = (tp + step) % n_tp
        return pltpu.make_async_remote_copy(
            src_ref=part.at[other],
            dst_ref=red.at[tp],
            send_sem=red_send.at[step],
            recv_sem=red_recv.at[tp],
            device_id={"tp": other, "seq": seq},
            device_id_type=MESH,
        )

    def project(g):
        place = g % per

        @pl.loop(1, n)
        def _(step):
            source = (me + step) % n
            share(per * tp + place, seq, source).wait_recv()

        gathered = mem[place].astype(jnp.float32)
        left = gathered[:, :picks].reshape(n * picks, half)
        right = gathered[:, picks:].reshape(n * picks, half)
        memory = jnp.concatenate((left, right), axis=1).astype(jnp.bfloat16)
        down_to = pl.multiple_of(place * columns, columns)
        for j in range(cols // tile):
            where = slice(j * tile, (j + 1) * tile)
            sums[:, where] += jnp.dot(
                memory, w_buf[pl.ds(down_to, columns), where], preferred_element_type=jnp.float32
            )

        @pl.when(place == per - 1)
        def _():
            part[...] = sums[...].reshape(n_tp, n_seq * picks, cols).astype(jnp.bfloat16)
            for step in range(1, n_tp):
                reduce(step).start()

    pl.semaphore_wait(barrier, n - 1)
    for c in range(AHEAD):
        own(c)
    q_copy.wait()
    w_copy.wait()

    @pl.loop(0, KV_HEADS + prior)
    def _(t):
        @pl.when(t + AHEAD < KV_HEADS)
        def _():
            own(t + AHEAD)

        for depth in range(1, prior + 1):
            c = t - (depth - 1)

            @pl.when((c >= 0) & (c < KV_HEADS))
            def _():
                from_below(c, depth)
                from_before(c, prior + 1 - depth)

        g = t - (prior - 1)

        @pl.when((g >= 0) & (g < KV_HEADS))
        def _():
            attend(g)
            each_share(g, lambda copy: copy.start())

            @pl.when(g // per == tp)
            def _():
                mem[g % per, me] = mine[g]

        @pl.when(g == KV_HEADS - 1)
        def _():
            meansq = jnp.sum(squares[...], axis=1, keepdims=True) / D
            scales[seq] = jnp.broadcast_to(lax.rsqrt(meansq + 1e-05), scales.shape[1:])
            for step in range(1, n_seq):
                scale_to(step).start()

        @pl.when((g >= 1) & ((g - 1) // per == tp))
        def _():
            project(g - 1)

    total = part[tp].astype(jnp.float32)
    for step in range(1, n_tp):
        source = (tp + step) % n_tp
        pltpu.make_async_remote_copy(
            src_ref=part.at[0],
            dst_ref=red.at[source],
            send_sem=red_send.at[step],
            recv_sem=red_recv.at[source],
            device_id={"tp": source, "seq": seq},
            device_id_type=MESH,
        ).wait_recv()
        total = total + red[source].astype(jnp.float32)
    for step in range(1, n_seq):
        source = (seq + step) % n_seq
        pltpu.make_async_remote_copy(
            src_ref=scales.at[source],
            dst_ref=scales.at[source],
            send_sem=scale_send.at[step],
            recv_sem=scale_recv.at[source],
            device_id={"tp": tp, "seq": source},
            device_id_type=MESH,
        ).wait_recv()
    factor = scales[...].reshape(n_seq * picks, HEAD_DIM)[:, :1]
    sum_ref[...] = (total * factor).astype(jnp.bfloat16)

    for step in range(1, n_tp):
        reduce(step).wait_send()
    for step in range(1, n_seq):
        scale_to(step).wait_send()

    @pl.loop(0, KV_HEADS)
    def _(g):
        each_share(g, lambda copy: copy.wait_send())

    @pl.loop(0, KV_HEADS)
    def _(c):
        @pl.when(has_up)
        def _():
            up(c, 0).wait_send()

        @pl.when(has_far)
        def _():
            far(c).wait_send()

        for k in range(1, prior):

            @pl.when((seq >= k) & has_up)
            def _():
                up(c, k).wait_send()

        for k in range(2, prior + 1):

            @pl.when((seq < k) & (tp > 0) & (seq >= 1))
            def _():
                down(c, k).wait_send()


def on_device(n_tp, n_seq, queries, keys, values, mem_pos, norm_gain, summary_weight):
    rows = queries.shape[0]
    picks = mem_pos.shape[0]
    prior = -(-(WINDOW - 1) // rows)
    n = n_tp * n_seq
    width = summary_weight.shape[0]
    cols = summary_weight.shape[1]
    per = KV_HEADS // n_tp
    half = width // per // 2
    vmem = pl.BlockSpec(memory_space=pltpu.VMEM)
    anywhere = pl.BlockSpec(memory_space=pl.ANY)
    bf16 = jnp.bfloat16
    dma = pltpu.SemaphoreType.DMA
    span = (prior + 1) * rows
    results = pl.pallas_call(
        functools.partial(kernel, n_tp, n_seq, prior),
        out_shape=(
            jax.ShapeDtypeStruct((rows, D), bf16),
            jax.ShapeDtypeStruct((n_seq * picks, cols), bf16),
        ),
        in_specs=[
            anywhere, vmem, vmem, pl.BlockSpec(memory_space=pltpu.SMEM), vmem, anywhere,
        ],
        out_specs=(vmem, vmem),
        scratch_shapes=[
            pltpu.VMEM((rows, D), bf16),
            pltpu.VMEM((width, cols), bf16),
            pltpu.VMEM((KV_HEADS, 2, span, HEAD_DIM), bf16),
            pltpu.VMEM((rows, span), jnp.float32),
            pltpu.VMEM((picks, HEAD_DIM), jnp.float32),
            pltpu.VMEM((KV_HEADS, 2 * picks, half), bf16),
            pltpu.VMEM((per, n, 2 * picks, half), bf16),
            pltpu.VMEM((n * picks, cols), jnp.float32),
            pltpu.VMEM((n_tp, n_seq * picks, cols), bf16),
            pltpu.VMEM((n_tp, n_seq * picks, cols), bf16),
            pltpu.VMEM((n_seq, picks, HEAD_DIM), jnp.float32),
            dma((2,)),
            dma((2, prior + 1, KV_HEADS)),
            dma((prior + 1, KV_HEADS)),
            dma((KV_HEADS, n_seq)),
            dma((per, n)),
            dma((n_tp,)),
            dma((n_tp,)),
            dma((n_seq,)),
            dma((n_seq,)),
        ],
        compiler_params=pltpu.CompilerParams(
            collective_id=0, has_side_effects=True, vmem_limit_bytes=60 * 1024 * 1024
        ),
        cost_estimate=pl.CostEstimate(
            flops=4 * HEADS * rows * span * HEAD_DIM + 2 * n * picks * width * cols,
            bytes_accessed=2 * (2 * rows * D + 4 * rows * KV_HEADS * HEAD_DIM + width * cols),
            transcendentals=HEADS * rows * span,
        ),
    )(queries, keys, values, mem_pos, norm_gain.reshape(1, D), summary_weight)
    return pl.pallas_call(
        hand_over,
        out_shape=tuple(jax.ShapeDtypeStruct(r.shape, r.dtype) for r in results),
        in_specs=[anywhere, anywhere],
        out_specs=(anywhere, anywhere),
        scratch_shapes=[
            *(pltpu.VMEM(r.shape, r.dtype) for r in results),
            dma((2, PIECES + 1)),
        ],
        compiler_params=pltpu.CompilerParams(vmem_limit_bytes=60 * 1024 * 1024),
    )(*results)


def solution(mesh):
    placed = (
        P(("file", "tp", "seq"), None),
        P(("file", "tp", "seq"), None),
        P(("file", "tp", "seq"), None),
        P(("file", "tp", "seq")),
        P(),
        P("tp", "seq"),
    )
    return jax.shard_map(
        functools.partial(on_device, mesh.shape["tp"], mesh.shape["seq"]),
        mesh=mesh,
        in_specs=placed,
        out_specs=(P(("file", "tp", "seq"), None), P(("file", "tp"), "seq")),
        check_vma=False,
    )
```

```python
import functools
import math

import jax
import jax.numpy as jnp
from jax import lax
from jax.experimental import pallas as pl
from jax.experimental.pallas import tpu as pltpu
from jax.sharding import PartitionSpec as P

D = 4096
HEADS = 32
KV_HEADS = 8
HEAD_DIM = 128
WINDOW = 512
SHARE = HEADS // KV_HEADS
MESH = pl.DeviceIdType.MESH
AHEAD = 3
PIECES = 4


def hand_over(enc_from, sum_from, enc_to, sum_to, enc_buf, sum_buf, sems):
    rows = enc_from.shape[0] // PIECES
    parts = [(sum_from, sum_buf, sum_to)]
    for i in range(PIECES):
        piece = pl.ds(i * rows, rows)
        parts.append((enc_from.at[piece], enc_buf.at[piece], enc_to.at[piece]))
    into = [pltpu.make_async_copy(a, b, sems.at[0, i]) for i, (a, b, c) in enumerate(parts)]
    out = [pltpu.make_async_copy(b, c, sems.at[1, i]) for i, (a, b, c) in enumerate(parts)]
    for copy in into:
        copy.start()
    for first, second in zip(into, out):
        first.wait()
        second.start()
    for copy in out:
        copy.wait()


def kernel(
    n_tp, n_seq, prior,
    q_hbm, k_ref, v_ref, pos_ref, gain_ref, w_hbm,
    enc_ref, sum_ref,
    q_buf, w_buf, kv, bias, help_bias, squares, mine, mem, sums, part, red, scales,
    help_q, help_out, returned,
    local_sem, kv_send, kv_recv, mem_send, mem_recv, red_send, red_recv, scale_send, scale_recv,
    query_send, query_recv, back_send, back_recv,
):
    tp = lax.axis_index("tp")
    seq = lax.axis_index("seq")
    me = tp * n_seq + seq
    n = n_tp * n_seq
    rows = k_ref.shape[0]
    span = (prior + 1) * rows
    picks = pos_ref.shape[0]
    per = KV_HEADS // n_tp
    columns = SHARE * HEAD_DIM
    half = columns // 2
    cols = sum_ref.shape[1]
    tile = 512 if cols % 512 == 0 else cols
    squares[...] = jnp.zeros_like(squares)
    sums[...] = jnp.zeros_like(sums)

    def device(index):
        return {"tp": index // n_seq, "seq": index % n_seq}

    is_top = seq == n_seq - 1
    is_bottom = (seq == 0) & (tp > 0)
    asks = is_top | is_bottom
    helps_top = seq == n_seq - 2
    helps_bottom = (seq == 1) & (tp > 0)
    helps = helps_top | helps_bottom
    inward = 1 - 2 * (seq // (n_seq - 1))
    outward = 2 * ((seq - 1) // (n_seq - 3)) - 1

    q_copy = pltpu.make_async_copy(q_hbm, q_buf, local_sem.at[0])
    w_copy = pltpu.make_async_copy(w_hbm, w_buf, local_sem.at[1])
    q_copy.start()
    w_copy.start()

    barrier = pltpu.get_barrier_semaphore()

    @pl.loop(1, n)
    def _(step):
        pl.semaphore_signal(
            barrier, inc=1, device_id=device((me + step) % n), device_id_type=MESH
        )

    for g in range(KV_HEADS):
        kv[g, 0, (prior + 1) * rows : (prior + 2) * rows, :] = k_ref[:, g * HEAD_DIM : (g + 1) * HEAD_DIM]
        kv[g, 1, (prior + 1) * rows : (prior + 2) * rows, :] = v_ref[:, g * HEAD_DIM : (g + 1) * HEAD_DIM]
    for k in range(1, prior + 1):

        @pl.when(me < k)
        def _():
            start = (prior + 1 - k) * rows
            kv[:, :, start : start + rows, :] = jnp.zeros(
                (KV_HEADS, 2, rows, HEAD_DIM), jnp.bfloat16
            )

    row = lax.broadcasted_iota(jnp.int32, (rows, span), 0)
    col = lax.broadcasted_iota(jnp.int32, (rows, span), 1) - prior * rows
    band = (col <= row) & (col > row - WINDOW)
    bias[...] = jnp.where(band & (col + me * rows >= 0), 0.0, -jnp.inf).astype(jnp.float32)
    help_seen = band & (col + (me + outward) * rows >= 0)
    help_bias[...] = jnp.where(help_seen, 0.0, -jnp.inf).astype(jnp.float32)

    pick_row = lax.broadcasted_iota(jnp.int32, (picks, rows), 0)
    pick_col = lax.broadcasted_iota(jnp.int32, (picks, rows), 1)
    wanted = jnp.zeros((picks, rows), jnp.int32)
    for j in range(picks):
        wanted = jnp.where(pick_row == j, pos_ref[j] - me * rows, wanted)
    choose = jnp.where(pick_col == wanted, 1.0, 0.0).astype(jnp.bfloat16)

    def slot(c, k):
        return kv.at[c, :, pl.ds((prior + 1 - k) * rows, rows), :]

    def send(c, k, lands, way, target):
        return pltpu.make_async_remote_copy(
            src_ref=slot(c, k),
            dst_ref=slot(c, lands),
            send_sem=kv_send.at[way, k, c],
            recv_sem=kv_recv.at[lands + 1, c],
            device_id=target,
            device_id_type=MESH,
        )

    def up(c, k):
        return send(c, k, k + 1, 0, {"tp": tp, "seq": seq + 1})

    def down(c, k):
        return send(c, k, k - 1, 1, {"tp": tp, "seq": seq - 1})

    def far(c):
        return send(c, 0, prior, 1, {"tp": tp + 1, "seq": seq + prior - n_seq})

    def extra_down(c):
        return send(c, 0, -1, 2, {"tp": tp, "seq": seq - 1})

    def extra_up(c):
        return send(c, prior, prior + 1, 2, {"tp": tp, "seq": seq + 1})

    def ask(c):
        return pltpu.make_async_remote_copy(
            src_ref=q_buf.at[:, pl.ds(pl.multiple_of(c * columns, columns), columns)],
            dst_ref=help_q.at[c // 2],
            send_sem=query_send.at[c // 2],
            recv_sem=query_recv.at[c // 2],
            device_id={"tp": tp, "seq": seq + inward},
            device_id_type=MESH,
        )

    def give_back(c):
        return pltpu.make_async_remote_copy(
            src_ref=help_out.at[c // 2],
            dst_ref=returned.at[c // 2],
            send_sem=back_send.at[c // 2],
            recv_sem=back_recv.at[c // 2],
            device_id={"tp": tp, "seq": seq + outward},
            device_id_type=MESH,
        )

    def has_up(c):
        return seq + 1 + c % 2 < n_seq

    def has_down(c):
        return seq >= 1 + c % 2

    has_far = (seq + prior >= n_seq) & (tp + 1 < n_tp)

    def each_own(c, act):
        @pl.when(has_up(c))
        def _():
            act(up(c, 0))

        @pl.when(has_far)
        def _():
            act(far(c))

        @pl.when(asks & (c % 2 == 1))
        def _():
            act(ask(c))

        @pl.when(is_top & (c % 2 == 1))
        def _():
            act(extra_down(c))

    def own(c):
        each_own(c, lambda copy: copy.start())

    def from_below(c, k):
        @pl.when((seq >= k) & (seq + c % 2 < n_seq))
        def _():
            up(c, k - 1).wait_recv()

            if k < prior:

                @pl.when(has_up(c))
                def _():
                    up(c, k).start()

        if k == 1:

            @pl.when(helps_top & (c % 2 == 1))
            def _():
                extra_down(c).wait_recv()

    def from_before(c, k):
        arrives = (seq < k) & (tp > 0)
        if k < prior:
            arrives = arrives & (seq >= c % 2)

        @pl.when(arrives)
        def _():
            send(c, 0, k, 1, {"tp": tp, "seq": seq}).wait_recv()

            if k >= 2:

                @pl.when(has_down(c))
                def _():
                    down(c, k).start()

            if k == prior:

                @pl.when(is_bottom & (c % 2 == 1))
                def _():
                    extra_up(c).start()

        if k == prior - 1:

            @pl.when(helps_bottom & (c % 2 == 1))
            def _():
                extra_up(c).wait_recv()

    fold = math.log2(math.e) / HEAD_DIM**0.5

    def attend(q_all, keys, values, bias):
        q_rows = jnp.concatenate(
            [q_all[:, h * HEAD_DIM : (h + 1) * HEAD_DIM] for h in range(SHARE)], axis=0
        )
        scores = lax.dot_general(
            q_rows, keys, (((1,), (1,)), ((), ())), preferred_element_type=jnp.float32
        )
        outs = []
        for h in range(SHARE):
            masked = scores[h * rows : (h + 1) * rows] + bias[...]
            peak = jnp.max(masked, axis=1, keepdims=True)
            weights = jnp.exp2((masked - peak) * fold)
            total = jnp.sum(weights, axis=1, keepdims=True)
            mixed = jnp.dot(
                weights.astype(jnp.bfloat16), values, preferred_element_type=jnp.float32
            )
            outs.append((mixed / total).astype(jnp.bfloat16))
        return jnp.concatenate(outs, axis=1)

    def encode(g):
        first = pl.multiple_of(g * columns, columns)
        theirs = asks & (g % 2 == 1)

        @pl.when(helps & (g % 2 == 1))
        def _():
            ask(g).wait_recv()
            reach = pl.ds(pl.multiple_of((1 + outward) * rows, rows), span)
            help_out[g // 2] = attend(
                help_q[g // 2], kv[g, 0, reach], kv[g, 1, reach], help_bias
            )
            give_back(g).start()

        @pl.when(jnp.logical_not(theirs))
        def _():
            enc_ref[:, pl.ds(first, columns)] = attend(
                q_buf[:, pl.ds(first, columns)],
                kv[g, 0, rows : rows + span],
                kv[g, 1, rows : rows + span],
                bias,
            )

        @pl.when(theirs)
        def _():
            give_back(g).wait_recv()
            enc_ref[:, pl.ds(first, columns)] = returned[g // 2]

        encoded = enc_ref[:, pl.ds(first, columns)]
        picked = jnp.dot(choose, encoded, preferred_element_type=jnp.float32)
        squared = picked * picked
        for h in range(SHARE):
            squares[...] += squared[:, h * HEAD_DIM : (h + 1) * HEAD_DIM]
        gained = picked * gain_ref[:, pl.ds(first, columns)]
        mine[g] = jnp.concatenate((gained[:, :half], gained[:, half:]), axis=0).astype(jnp.bfloat16)

    def share(g, s, source):
        return pltpu.make_async_remote_copy(
            src_ref=mine.at[g],
            dst_ref=mem.at[g % per, source],
            send_sem=mem_send.at[g, s],
            recv_sem=mem_recv.at[g % per, source],
            device_id={"tp": g // per, "seq": s},
            device_id_type=MESH,
        )

    def each_share(g, act):
        for step in range(1, n_seq):
            act(share(g, (seq + step) % n_seq, me))

        @pl.when(g // per != tp)
        def _():
            act(share(g, seq, me))

    def scale_to(step):
        return pltpu.make_async_remote_copy(
            src_ref=scales.at[seq],
            dst_ref=scales.at[seq],
            send_sem=scale_send.at[step],
            recv_sem=scale_recv.at[seq],
            device_id={"tp": tp, "seq": (seq + step) % n_seq},
            device_id_type=MESH,
        )

    def reduce(step):
        other = (tp + step) % n_tp
        return pltpu.make_async_remote_copy(
            src_ref=part.at[other],
            dst_ref=red.at[tp],
            send_sem=red_send.at[step],
            recv_sem=red_recv.at[tp],
            device_id={"tp": other, "seq": seq},
            device_id_type=MESH,
        )

    def project(g):
        place = g % per

        @pl.loop(1, n)
        def _(step):
            source = (me + step) % n
            share(per * tp + place, seq, source).wait_recv()

        gathered = mem[place].astype(jnp.float32)
        left = gathered[:, :picks].reshape(n * picks, half)
        right = gathered[:, picks:].reshape(n * picks, half)
        memory = jnp.concatenate((left, right), axis=1).astype(jnp.bfloat16)
        down_to = pl.multiple_of(place * columns, columns)
        for j in range(cols // tile):
            where = slice(j * tile, (j + 1) * tile)
            sums[:, where] += jnp.dot(
                memory, w_buf[pl.ds(down_to, columns), where], preferred_element_type=jnp.float32
            )

        @pl.when(place == per - 1)
        def _():
            part[...] = sums[...].reshape(n_tp, n_seq * picks, cols).astype(jnp.bfloat16)
            for step in range(1, n_tp):
                reduce(step).start()

    pl.semaphore_wait(barrier, n - 1)
    q_copy.wait()
    for c in range(AHEAD):
        own(c)
    w_copy.wait()

    @pl.loop(0, KV_HEADS + prior)
    def _(t):
        @pl.when(t + AHEAD < KV_HEADS)
        def _():
            own(t + AHEAD)

        for depth in range(1, prior + 1):
            c = t - (depth - 1)

            @pl.when((c >= 0) & (c < KV_HEADS))
            def _():
                from_below(c, depth)
                from_before(c, prior + 1 - depth)

        g = t - (prior - 1)

        @pl.when((g >= 0) & (g < KV_HEADS))
        def _():
            encode(g)
            each_share(g, lambda copy: copy.start())

            @pl.when(g // per == tp)
            def _():
                mem[g % per, me] = mine[g]

        @pl.when(g == KV_HEADS - 1)
        def _():
            meansq = jnp.sum(squares[...], axis=1, keepdims=True) / D
            scales[seq] = jnp.broadcast_to(lax.rsqrt(meansq + 1e-05), scales.shape[1:])
            for step in range(1, n_seq):
                scale_to(step).start()

        @pl.when((g >= 1) & ((g - 1) // per == tp))
        def _():
            project(g - 1)

    total = part[tp].astype(jnp.float32)
    for step in range(1, n_tp):
        source = (tp + step) % n_tp
        pltpu.make_async_remote_copy(
            src_ref=part.at[0],
            dst_ref=red.at[source],
            send_sem=red_send.at[step],
            recv_sem=red_recv.at[source],
            device_id={"tp": source, "seq": seq},
            device_id_type=MESH,
        ).wait_recv()
        total = total + red[source].astype(jnp.float32)
    for step in range(1, n_seq):
        source = (seq + step) % n_seq
        pltpu.make_async_remote_copy(
            src_ref=scales.at[source],
            dst_ref=scales.at[source],
            send_sem=scale_send.at[step],
            recv_sem=scale_recv.at[source],
            device_id={"tp": tp, "seq": source},
            device_id_type=MESH,
        ).wait_recv()
    factor = scales[...].reshape(n_seq * picks, HEAD_DIM)[:, :1]
    sum_ref[...] = (total * factor).astype(jnp.bfloat16)

    for step in range(1, n_tp):
        reduce(step).wait_send()
    for step in range(1, n_seq):
        scale_to(step).wait_send()

    @pl.loop(0, KV_HEADS)
    def _(g):
        each_share(g, lambda copy: copy.wait_send())

    @pl.loop(0, KV_HEADS)
    def _(c):
        each_own(c, lambda copy: copy.wait_send())

        for k in range(1, prior):

            @pl.when((seq >= k) & has_up(c))
            def _():
                up(c, k).wait_send()

        for k in range(2, prior + 1):

            @pl.when((seq < k) & (tp > 0) & has_down(c))
            def _():
                down(c, k).wait_send()

        @pl.when(is_bottom & (c % 2 == 1))
        def _():
            extra_up(c).wait_send()

        @pl.when(helps & (c % 2 == 1))
        def _():
            give_back(c).wait_send()


def on_device(n_tp, n_seq, queries, keys, values, mem_pos, norm_gain, summary_weight):
    rows = queries.shape[0]
    picks = mem_pos.shape[0]
    prior = -(-(WINDOW - 1) // rows)
    n = n_tp * n_seq
    width = summary_weight.shape[0]
    cols = summary_weight.shape[1]
    per = KV_HEADS // n_tp
    half = width // per // 2
    vmem = pl.BlockSpec(memory_space=pltpu.VMEM)
    anywhere = pl.BlockSpec(memory_space=pl.ANY)
    bf16 = jnp.bfloat16
    dma = pltpu.SemaphoreType.DMA
    span = (prior + 1) * rows
    results = pl.pallas_call(
        functools.partial(kernel, n_tp, n_seq, prior),
        out_shape=(
            jax.ShapeDtypeStruct((rows, D), bf16),
            jax.ShapeDtypeStruct((n_seq * picks, cols), bf16),
        ),
        in_specs=[
            anywhere, vmem, vmem, pl.BlockSpec(memory_space=pltpu.SMEM), vmem, anywhere,
        ],
        out_specs=(vmem, vmem),
        scratch_shapes=[
            pltpu.VMEM((rows, D), bf16),
            pltpu.VMEM((width, cols), bf16),
            pltpu.VMEM((KV_HEADS, 2, (prior + 3) * rows, HEAD_DIM), bf16),
            pltpu.VMEM((rows, span), jnp.float32),
            pltpu.VMEM((rows, span), jnp.float32),
            pltpu.VMEM((picks, HEAD_DIM), jnp.float32),
            pltpu.VMEM((KV_HEADS, 2 * picks, half), bf16),
            pltpu.VMEM((per, n, 2 * picks, half), bf16),
            pltpu.VMEM((n * picks, cols), jnp.float32),
            pltpu.VMEM((n_tp, n_seq * picks, cols), bf16),
            pltpu.VMEM((n_tp, n_seq * picks, cols), bf16),
            pltpu.VMEM((n_seq, picks, HEAD_DIM), jnp.float32),
            pltpu.VMEM((KV_HEADS // 2, rows, D // KV_HEADS), bf16),
            pltpu.VMEM((KV_HEADS // 2, rows, D // KV_HEADS), bf16),
            pltpu.VMEM((KV_HEADS // 2, rows, D // KV_HEADS), bf16),
            dma((2,)),
            dma((3, prior + 1, KV_HEADS)),
            dma((prior + 3, KV_HEADS)),
            dma((KV_HEADS, n_seq)),
            dma((per, n)),
            dma((n_tp,)),
            dma((n_tp,)),
            dma((n_seq,)),
            dma((n_seq,)),
            dma((KV_HEADS // 2,)),
            dma((KV_HEADS // 2,)),
            dma((KV_HEADS // 2,)),
            dma((KV_HEADS // 2,)),
        ],
        compiler_params=pltpu.CompilerParams(
            collective_id=0, has_side_effects=True, vmem_limit_bytes=60 * 1024 * 1024
        ),
        cost_estimate=pl.CostEstimate(
            flops=4 * HEADS * rows * span * HEAD_DIM + 2 * n * picks * width * cols,
            bytes_accessed=2 * (2 * rows * D + 4 * rows * KV_HEADS * HEAD_DIM + width * cols),
            transcendentals=HEADS * rows * span,
        ),
    )(queries, keys, values, mem_pos, norm_gain.reshape(1, D), summary_weight)
    return pl.pallas_call(
        hand_over,
        out_shape=tuple(jax.ShapeDtypeStruct(r.shape, r.dtype) for r in results),
        in_specs=[anywhere, anywhere],
        out_specs=(anywhere, anywhere),
        scratch_shapes=[
            *(pltpu.VMEM(r.shape, r.dtype) for r in results),
            dma((2, PIECES + 1)),
        ],
        compiler_params=pltpu.CompilerParams(vmem_limit_bytes=60 * 1024 * 1024),
    )(*results)


def solution(mesh):
    placed = (
        P(("file", "tp", "seq"), None),
        P(("file", "tp", "seq"), None),
        P(("file", "tp", "seq"), None),
        P(("file", "tp", "seq")),
        P(),
        P("tp", "seq"),
    )
    return jax.shard_map(
        functools.partial(on_device, mesh.shape["tp"], mesh.shape["seq"]),
        mesh=mesh,
        in_specs=placed,
        out_specs=(P(("file", "tp", "seq"), None), P(("file", "tp"), "seq")),
        check_vma=False,
    )
```

```python
import functools
import math

import jax
import jax.numpy as jnp
from jax import lax
from jax.experimental import pallas as pl
from jax.experimental.pallas import tpu as pltpu
from jax.sharding import PartitionSpec as P

D = 4096
HEADS = 32
KV_HEADS = 8
HEAD_DIM = 128
WINDOW = 512
SHARE = HEADS // KV_HEADS
MESH = pl.DeviceIdType.MESH
AHEAD = 3
PIECES = 4


def hand_over(enc_from, sum_from, enc_to, sum_to, enc_buf, sum_buf, sems):
    rows = enc_from.shape[0] // PIECES
    parts = [(sum_from, sum_buf, sum_to)]
    for i in range(PIECES):
        piece = pl.ds(i * rows, rows)
        parts.append((enc_from.at[piece], enc_buf.at[piece], enc_to.at[piece]))
    into = [pltpu.make_async_copy(a, b, sems.at[0, i]) for i, (a, b, c) in enumerate(parts)]
    out = [pltpu.make_async_copy(b, c, sems.at[1, i]) for i, (a, b, c) in enumerate(parts)]
    for copy in into:
        copy.start()
    for first, second in zip(into, out):
        first.wait()
        second.start()
    for copy in out:
        copy.wait()


def kernel(
    n_tp, n_seq, prior,
    q_hbm, k_ref, v_ref, pos_ref, gain_ref, w_hbm,
    enc_ref, sum_ref,
    q_buf, w_buf, kv, bias, squares, mine, mem, sums, part, red, scales,
    local_sem, kv_send, kv_recv, mem_send, mem_recv, red_send, red_recv, scale_send, scale_recv,
):
    tp = lax.axis_index("tp")
    seq = lax.axis_index("seq")
    me = tp * n_seq + seq
    n = n_tp * n_seq
    rows = k_ref.shape[0]
    assert rows == HEAD_DIM
    span = (prior + 1) * rows
    picks = pos_ref.shape[0]
    per = KV_HEADS // n_tp
    columns = SHARE * HEAD_DIM
    half = columns // 2
    cols = sum_ref.shape[1]
    tile = 512 if cols % 512 == 0 else cols
    squares[...] = jnp.zeros_like(squares)
    sums[...] = jnp.zeros_like(sums)

    def device(index):
        return {"tp": index // n_seq, "seq": index % n_seq}

    q_copy = pltpu.make_async_copy(q_hbm, q_buf, local_sem.at[0])
    w_copy = pltpu.make_async_copy(w_hbm, w_buf, local_sem.at[1])
    q_copy.start()
    w_copy.start()

    barrier = pltpu.get_barrier_semaphore()

    @pl.loop(1, n)
    def _(step):
        pl.semaphore_signal(
            barrier, inc=1, device_id=device((me + step) % n), device_id_type=MESH
        )

    for g in range(KV_HEADS):
        kv[g, 0, prior * rows :, :] = k_ref[:, g * HEAD_DIM : (g + 1) * HEAD_DIM]
        kv[g, 1, prior * rows :, :] = v_ref[:, g * HEAD_DIM : (g + 1) * HEAD_DIM].T
    for k in range(1, prior + 1):

        @pl.when(me < k)
        def _():
            start = (prior - k) * rows
            kv[:, :, start : start + rows, :] = jnp.zeros(
                (KV_HEADS, 2, rows, HEAD_DIM), jnp.bfloat16
            )

    row = lax.broadcasted_iota(jnp.int32, (span, rows), 1)
    col = lax.broadcasted_iota(jnp.int32, (span, rows), 0) - prior * rows
    seen = (col <= row) & (col > row - WINDOW) & (col + me * rows >= 0)
    bias[...] = jnp.where(seen, 0.0, -jnp.inf).astype(jnp.float32)

    pick_row = lax.broadcasted_iota(jnp.int32, (picks, rows), 0)
    pick_col = lax.broadcasted_iota(jnp.int32, (picks, rows), 1)
    wanted = jnp.zeros((picks, rows), jnp.int32)
    for j in range(picks):
        wanted = jnp.where(pick_row == j, pos_ref[j] - me * rows, wanted)
    choose = jnp.where(pick_col == wanted, 1.0, 0.0).astype(jnp.bfloat16)

    def slot(c, k):
        return kv.at[c, :, pl.ds((prior - k) * rows, rows), :]

    def send(c, k, lands, way, target):
        return pltpu.make_async_remote_copy(
            src_ref=slot(c, k),
            dst_ref=slot(c, lands),
            send_sem=kv_send.at[way, k, c],
            recv_sem=kv_recv.at[lands, c],
            device_id=target,
            device_id_type=MESH,
        )

    def up(c, k):
        return send(c, k, k + 1, 0, {"tp": tp, "seq": seq + 1})

    def down(c, k):
        return send(c, k, k - 1, 1, {"tp": tp, "seq": seq - 1})

    def far(c):
        return send(c, 0, prior, 1, {"tp": tp + 1, "seq": seq + prior - n_seq})

    has_up = seq + 1 < n_seq
    has_far = (seq + prior >= n_seq) & (tp + 1 < n_tp)

    def own(c):
        @pl.when(has_up)
        def _():
            up(c, 0).start()

        @pl.when(has_far)
        def _():
            far(c).start()

    def from_below(c, k):
        @pl.when(seq >= k)
        def _():
            up(c, k - 1).wait_recv()

            if k < prior:

                @pl.when(has_up)
                def _():
                    up(c, k).start()

    def from_before(c, k):
        @pl.when((seq < k) & (tp > 0))
        def _():
            send(c, 0, k, 1, {"tp": tp, "seq": seq}).wait_recv()

            if k >= 2:

                @pl.when(seq >= 1)
                def _():
                    down(c, k).start()

    fold = math.log2(math.e) / HEAD_DIM**0.5

    def attend(q_all, keys, flipped, bias):
        q_rows = jnp.concatenate(
            [q_all[:, h * HEAD_DIM : (h + 1) * HEAD_DIM] for h in range(SHARE)], axis=0
        )
        scores = lax.dot_general(
            keys, q_rows, (((1,), (1,)), ((), ())), preferred_element_type=jnp.float32
        )
        masked = scores + jnp.concatenate([bias[...]] * SHARE, axis=1)
        peak = jnp.max(masked, axis=0, keepdims=True)
        weights = jnp.exp2((masked - peak) * fold)
        total = jnp.sum(weights, axis=0, keepdims=True)
        values = jnp.concatenate(
            [flipped[b * rows : (b + 1) * rows] for b in range(prior + 1)], axis=1
        )
        mixed = jnp.dot(values, weights.astype(jnp.bfloat16), preferred_element_type=jnp.float32)
        mixed = mixed * (1.0 / total)
        return jnp.concatenate(
            [mixed[:, h * rows : (h + 1) * rows].T for h in range(SHARE)], axis=1
        ).astype(jnp.bfloat16)

    def encode(g):
        first = pl.multiple_of(g * columns, columns)
        encoded = attend(q_buf[:, pl.ds(first, columns)], kv[g, 0], kv[g, 1], bias)
        enc_ref[:, pl.ds(first, columns)] = encoded
        picked = jnp.dot(choose, encoded, preferred_element_type=jnp.float32)
        squared = picked * picked
        for h in range(SHARE):
            squares[...] += squared[:, h * HEAD_DIM : (h + 1) * HEAD_DIM]
        gained = picked * gain_ref[:, pl.ds(first, columns)]
        mine[g] = jnp.concatenate((gained[:, :half], gained[:, half:]), axis=0).astype(jnp.bfloat16)

    def share(g, s, source):
        return pltpu.make_async_remote_copy(
            src_ref=mine.at[g],
            dst_ref=mem.at[g % per, source],
            send_sem=mem_send.at[g, s],
            recv_sem=mem_recv.at[g % per, source],
            device_id={"tp": g // per, "seq": s},
            device_id_type=MESH,
        )

    def each_share(g, act):
        for step in range(1, n_seq):
            act(share(g, (seq + step) % n_seq, me))

        @pl.when(g // per != tp)
        def _():
            act(share(g, seq, me))

    def scale_to(step):
        return pltpu.make_async_remote_copy(
            src_ref=scales.at[seq],
            dst_ref=scales.at[seq],
            send_sem=scale_send.at[step],
            recv_sem=scale_recv.at[seq],
            device_id={"tp": tp, "seq": (seq + step) % n_seq},
            device_id_type=MESH,
        )

    def reduce(step):
        other = (tp + step) % n_tp
        return pltpu.make_async_remote_copy(
            src_ref=part.at[other],
            dst_ref=red.at[tp],
            send_sem=red_send.at[step],
            recv_sem=red_recv.at[tp],
            device_id={"tp": other, "seq": seq},
            device_id_type=MESH,
        )

    def project(g):
        place = g % per

        @pl.loop(1, n)
        def _(step):
            source = (me + step) % n
            share(per * tp + place, seq, source).wait_recv()

        gathered = mem[place].astype(jnp.float32)
        left = gathered[:, :picks].reshape(n * picks, half)
        right = gathered[:, picks:].reshape(n * picks, half)
        memory = jnp.concatenate((left, right), axis=1).astype(jnp.bfloat16)
        down_to = pl.multiple_of(place * columns, columns)
        for j in range(cols // tile):
            where = slice(j * tile, (j + 1) * tile)
            sums[:, where] += jnp.dot(
                memory, w_buf[pl.ds(down_to, columns), where], preferred_element_type=jnp.float32
            )

        @pl.when(place == per - 1)
        def _():
            part[...] = sums[...].reshape(n_tp, n_seq * picks, cols).astype(jnp.bfloat16)
            for step in range(1, n_tp):
                reduce(step).start()

    pl.semaphore_wait(barrier, n - 1)
    for c in range(AHEAD):
        own(c)
    q_copy.wait()
    w_copy.wait()

    @pl.loop(0, KV_HEADS + prior)
    def _(t):
        @pl.when(t + AHEAD < KV_HEADS)
        def _():
            own(t + AHEAD)

        for depth in range(1, prior + 1):
            c = t - (depth - 1)

            @pl.when((c >= 0) & (c < KV_HEADS))
            def _():
                from_below(c, depth)
                from_before(c, prior + 1 - depth)

        g = t - (prior - 1)

        @pl.when((g >= 0) & (g < KV_HEADS))
        def _():
            encode(g)
            each_share(g, lambda copy: copy.start())

            @pl.when(g // per == tp)
            def _():
                mem[g % per, me] = mine[g]

        @pl.when(g == KV_HEADS - 1)
        def _():
            meansq = jnp.sum(squares[...], axis=1, keepdims=True) / D
            scales[seq] = jnp.broadcast_to(lax.rsqrt(meansq + 1e-05), scales.shape[1:])
            for step in range(1, n_seq):
                scale_to(step).start()

        @pl.when((g >= 1) & ((g - 1) // per == tp))
        def _():
            project(g - 1)

    total = part[tp].astype(jnp.float32)
    for step in range(1, n_tp):
        source = (tp + step) % n_tp
        pltpu.make_async_remote_copy(
            src_ref=part.at[0],
            dst_ref=red.at[source],
            send_sem=red_send.at[step],
            recv_sem=red_recv.at[source],
            device_id={"tp": source, "seq": seq},
            device_id_type=MESH,
        ).wait_recv()
        total = total + red[source].astype(jnp.float32)
    for step in range(1, n_seq):
        source = (seq + step) % n_seq
        pltpu.make_async_remote_copy(
            src_ref=scales.at[source],
            dst_ref=scales.at[source],
            send_sem=scale_send.at[step],
            recv_sem=scale_recv.at[source],
            device_id={"tp": tp, "seq": source},
            device_id_type=MESH,
        ).wait_recv()
    factor = scales[...].reshape(n_seq * picks, HEAD_DIM)[:, :1]
    sum_ref[...] = (total * factor).astype(jnp.bfloat16)

    for step in range(1, n_tp):
        reduce(step).wait_send()
    for step in range(1, n_seq):
        scale_to(step).wait_send()

    @pl.loop(0, KV_HEADS)
    def _(g):
        each_share(g, lambda copy: copy.wait_send())

    @pl.loop(0, KV_HEADS)
    def _(c):
        @pl.when(has_up)
        def _():
            up(c, 0).wait_send()

        @pl.when(has_far)
        def _():
            far(c).wait_send()

        for k in range(1, prior):

            @pl.when((seq >= k) & has_up)
            def _():
                up(c, k).wait_send()

        for k in range(2, prior + 1):

            @pl.when((seq < k) & (tp > 0) & (seq >= 1))
            def _():
                down(c, k).wait_send()


def on_device(n_tp, n_seq, queries, keys, values, mem_pos, norm_gain, summary_weight):
    rows = queries.shape[0]
    picks = mem_pos.shape[0]
    prior = -(-(WINDOW - 1) // rows)
    n = n_tp * n_seq
    width = summary_weight.shape[0]
    cols = summary_weight.shape[1]
    per = KV_HEADS // n_tp
    half = width // per // 2
    vmem = pl.BlockSpec(memory_space=pltpu.VMEM)
    anywhere = pl.BlockSpec(memory_space=pl.ANY)
    bf16 = jnp.bfloat16
    dma = pltpu.SemaphoreType.DMA
    span = (prior + 1) * rows
    results = pl.pallas_call(
        functools.partial(kernel, n_tp, n_seq, prior),
        out_shape=(
            jax.ShapeDtypeStruct((rows, D), bf16),
            jax.ShapeDtypeStruct((n_seq * picks, cols), bf16),
        ),
        in_specs=[
            anywhere, vmem, vmem, pl.BlockSpec(memory_space=pltpu.SMEM), vmem, anywhere,
        ],
        out_specs=(vmem, vmem),
        scratch_shapes=[
            pltpu.VMEM((rows, D), bf16),
            pltpu.VMEM((width, cols), bf16),
            pltpu.VMEM((KV_HEADS, 2, span, HEAD_DIM), bf16),
            pltpu.VMEM((span, rows), jnp.float32),
            pltpu.VMEM((picks, HEAD_DIM), jnp.float32),
            pltpu.VMEM((KV_HEADS, 2 * picks, half), bf16),
            pltpu.VMEM((per, n, 2 * picks, half), bf16),
            pltpu.VMEM((n * picks, cols), jnp.float32),
            pltpu.VMEM((n_tp, n_seq * picks, cols), bf16),
            pltpu.VMEM((n_tp, n_seq * picks, cols), bf16),
            pltpu.VMEM((n_seq, picks, HEAD_DIM), jnp.float32),
            dma((2,)),
            dma((2, prior + 1, KV_HEADS)),
            dma((prior + 1, KV_HEADS)),
            dma((KV_HEADS, n_seq)),
            dma((per, n)),
            dma((n_tp,)),
            dma((n_tp,)),
            dma((n_seq,)),
            dma((n_seq,)),
        ],
        compiler_params=pltpu.CompilerParams(
            collective_id=0, has_side_effects=True, vmem_limit_bytes=60 * 1024 * 1024
        ),
        cost_estimate=pl.CostEstimate(
            flops=4 * HEADS * rows * span * HEAD_DIM + 2 * n * picks * width * cols,
            bytes_accessed=2 * (2 * rows * D + 4 * rows * KV_HEADS * HEAD_DIM + width * cols),
            transcendentals=HEADS * rows * span,
        ),
    )(queries, keys, values, mem_pos, norm_gain.reshape(1, D), summary_weight)
    return pl.pallas_call(
        hand_over,
        out_shape=tuple(jax.ShapeDtypeStruct(r.shape, r.dtype) for r in results),
        in_specs=[anywhere, anywhere],
        out_specs=(anywhere, anywhere),
        scratch_shapes=[
            *(pltpu.VMEM(r.shape, r.dtype) for r in results),
            dma((2, PIECES + 1)),
        ],
        compiler_params=pltpu.CompilerParams(vmem_limit_bytes=60 * 1024 * 1024),
    )(*results)


def solution(mesh):
    placed = (
        P(("file", "tp", "seq"), None),
        P(("file", "tp", "seq"), None),
        P(("file", "tp", "seq"), None),
        P(("file", "tp", "seq")),
        P(),
        P("tp", "seq"),
    )
    return jax.shard_map(
        functools.partial(on_device, mesh.shape["tp"], mesh.shape["seq"]),
        mesh=mesh,
        in_specs=placed,
        out_specs=(P(("file", "tp", "seq"), None), P(("file", "tp"), "seq")),
        check_vma=False,
    )
```

```python
import functools
import math

import jax
import jax.numpy as jnp
from jax import lax
from jax.experimental import pallas as pl
from jax.experimental.pallas import tpu as pltpu
from jax.sharding import PartitionSpec as P

D = 4096
HEADS = 32
KV_HEADS = 8
HEAD_DIM = 128
WINDOW = 512
SHARE = HEADS // KV_HEADS
MESH = pl.DeviceIdType.MESH
AHEAD = 3
PIECES = 4


def hand_over(enc_from, sum_from, enc_to, sum_to, enc_buf, sum_buf, sems):
    rows = enc_from.shape[0] // PIECES
    parts = [(sum_from, sum_buf, sum_to)]
    for i in range(PIECES):
        piece = pl.ds(i * rows, rows)
        parts.append((enc_from.at[piece], enc_buf.at[piece], enc_to.at[piece]))
    into = [pltpu.make_async_copy(a, b, sems.at[0, i]) for i, (a, b, c) in enumerate(parts)]
    out = [pltpu.make_async_copy(b, c, sems.at[1, i]) for i, (a, b, c) in enumerate(parts)]
    for copy in into:
        copy.start()
    for first, second in zip(into, out):
        first.wait()
        second.start()
    for copy in out:
        copy.wait()


def kernel(
    n_tp, n_seq, prior,
    q_hbm, k_ref, v_ref, pos_ref, gain_ref, w_hbm,
    enc_ref, sum_ref,
    q_buf, w_buf, kv, bias, help_bias, squares, mine, mem, sums, part, red, scales,
    help_q, help_out, returned,
    local_sem, kv_send, kv_recv, mem_send, mem_recv, red_send, red_recv, scale_send, scale_recv,
    query_send, query_recv, back_send, back_recv,
):
    tp = lax.axis_index("tp")
    seq = lax.axis_index("seq")
    me = tp * n_seq + seq
    n = n_tp * n_seq
    rows = k_ref.shape[0]
    assert rows == HEAD_DIM
    span = (prior + 1) * rows
    picks = pos_ref.shape[0]
    per = KV_HEADS // n_tp
    columns = SHARE * HEAD_DIM
    half = columns // 2
    cols = sum_ref.shape[1]
    tile = 512 if cols % 512 == 0 else cols
    squares[...] = jnp.zeros_like(squares)
    sums[...] = jnp.zeros_like(sums)

    def device(index):
        return {"tp": index // n_seq, "seq": index % n_seq}

    is_top = seq == n_seq - 1
    is_bottom = (seq == 0) & (tp > 0)
    asks = is_top | is_bottom
    helps_top = seq == n_seq - 2
    helps_bottom = (seq == 1) & (tp > 0)
    helps = helps_top | helps_bottom
    inward = 1 - 2 * (seq // (n_seq - 1))
    outward = 2 * ((seq - 1) // (n_seq - 3)) - 1

    q_copy = pltpu.make_async_copy(q_hbm, q_buf, local_sem.at[0])
    w_copy = pltpu.make_async_copy(w_hbm, w_buf, local_sem.at[1])
    q_copy.start()
    w_copy.start()

    barrier = pltpu.get_barrier_semaphore()

    @pl.loop(1, n)
    def _(step):
        pl.semaphore_signal(
            barrier, inc=1, device_id=device((me + step) % n), device_id_type=MESH
        )

    for g in range(KV_HEADS):
        kv[g, 0, (prior + 1) * rows : (prior + 2) * rows, :] = k_ref[:, g * HEAD_DIM : (g + 1) * HEAD_DIM]
        kv[g, 1, (prior + 1) * rows : (prior + 2) * rows, :] = v_ref[:, g * HEAD_DIM : (g + 1) * HEAD_DIM].T
    for k in range(1, prior + 1):

        @pl.when(me < k)
        def _():
            start = (prior + 1 - k) * rows
            kv[:, :, start : start + rows, :] = jnp.zeros(
                (KV_HEADS, 2, rows, HEAD_DIM), jnp.bfloat16
            )

    row = lax.broadcasted_iota(jnp.int32, (span, rows), 1)
    col = lax.broadcasted_iota(jnp.int32, (span, rows), 0) - prior * rows
    band = (col <= row) & (col > row - WINDOW)
    bias[...] = jnp.where(band & (col + me * rows >= 0), 0.0, -jnp.inf).astype(jnp.float32)
    help_seen = band & (col + (me + outward) * rows >= 0)
    help_bias[...] = jnp.where(help_seen, 0.0, -jnp.inf).astype(jnp.float32)

    pick_row = lax.broadcasted_iota(jnp.int32, (picks, rows), 0)
    pick_col = lax.broadcasted_iota(jnp.int32, (picks, rows), 1)
    wanted = jnp.zeros((picks, rows), jnp.int32)
    for j in range(picks):
        wanted = jnp.where(pick_row == j, pos_ref[j] - me * rows, wanted)
    choose = jnp.where(pick_col == wanted, 1.0, 0.0).astype(jnp.bfloat16)

    def slot(c, k):
        return kv.at[c, :, pl.ds((prior + 1 - k) * rows, rows), :]

    def send(c, k, lands, way, target):
        return pltpu.make_async_remote_copy(
            src_ref=slot(c, k),
            dst_ref=slot(c, lands),
            send_sem=kv_send.at[way, k, c],
            recv_sem=kv_recv.at[lands + 1, c],
            device_id=target,
            device_id_type=MESH,
        )

    def up(c, k):
        return send(c, k, k + 1, 0, {"tp": tp, "seq": seq + 1})

    def down(c, k):
        return send(c, k, k - 1, 1, {"tp": tp, "seq": seq - 1})

    def far(c):
        return send(c, 0, prior, 1, {"tp": tp + 1, "seq": seq + prior - n_seq})

    def extra_down(c):
        return send(c, 0, -1, 2, {"tp": tp, "seq": seq - 1})

    def extra_up(c):
        return send(c, prior, prior + 1, 2, {"tp": tp, "seq": seq + 1})

    def ask(c):
        return pltpu.make_async_remote_copy(
            src_ref=q_buf.at[:, pl.ds(pl.multiple_of(c * columns, columns), columns)],
            dst_ref=help_q.at[c // 2],
            send_sem=query_send.at[c // 2],
            recv_sem=query_recv.at[c // 2],
            device_id={"tp": tp, "seq": seq + inward},
            device_id_type=MESH,
        )

    def give_back(c):
        return pltpu.make_async_remote_copy(
            src_ref=help_out.at[c // 2],
            dst_ref=returned.at[c // 2],
            send_sem=back_send.at[c // 2],
            recv_sem=back_recv.at[c // 2],
            device_id={"tp": tp, "seq": seq + outward},
            device_id_type=MESH,
        )

    def has_up(c):
        return seq + 1 + c % 2 < n_seq

    def has_down(c):
        return seq >= 1 + c % 2

    has_far = (seq + prior >= n_seq) & (tp + 1 < n_tp)

    def each_own(c, act):
        @pl.when(has_up(c))
        def _():
            act(up(c, 0))

        @pl.when(has_far)
        def _():
            act(far(c))

        @pl.when(asks & (c % 2 == 1))
        def _():
            act(ask(c))

        @pl.when(is_top & (c % 2 == 1))
        def _():
            act(extra_down(c))

    def own(c):
        each_own(c, lambda copy: copy.start())

    def from_below(c, k):
        @pl.when((seq >= k) & (seq + c % 2 < n_seq))
        def _():
            up(c, k - 1).wait_recv()

            if k < prior:

                @pl.when(has_up(c))
                def _():
                    up(c, k).start()

        if k == 1:

            @pl.when(helps_top & (c % 2 == 1))
            def _():
                extra_down(c).wait_recv()

    def from_before(c, k):
        arrives = (seq < k) & (tp > 0)
        if k < prior:
            arrives = arrives & (seq >= c % 2)

        @pl.when(arrives)
        def _():
            send(c, 0, k, 1, {"tp": tp, "seq": seq}).wait_recv()

            if k >= 2:

                @pl.when(has_down(c))
                def _():
                    down(c, k).start()

            if k == prior:

                @pl.when(is_bottom & (c % 2 == 1))
                def _():
                    extra_up(c).start()

        if k == prior - 1:

            @pl.when(helps_bottom & (c % 2 == 1))
            def _():
                extra_up(c).wait_recv()

    fold = math.log2(math.e) / HEAD_DIM**0.5

    def attend(q_all, keys, flipped, bias):
        q_rows = jnp.concatenate(
            [q_all[:, h * HEAD_DIM : (h + 1) * HEAD_DIM] for h in range(SHARE)], axis=0
        )
        scores = lax.dot_general(
            keys, q_rows, (((1,), (1,)), ((), ())), preferred_element_type=jnp.float32
        )
        masked = scores + jnp.concatenate([bias[...]] * SHARE, axis=1)
        peak = jnp.max(masked, axis=0, keepdims=True)
        weights = jnp.exp2((masked - peak) * fold)
        total = jnp.sum(weights, axis=0, keepdims=True)
        values = jnp.concatenate(
            [flipped[b * rows : (b + 1) * rows] for b in range(prior + 1)], axis=1
        )
        mixed = jnp.dot(values, weights.astype(jnp.bfloat16), preferred_element_type=jnp.float32)
        mixed = mixed * (1.0 / total)
        return jnp.concatenate(
            [mixed[:, h * rows : (h + 1) * rows].T for h in range(SHARE)], axis=1
        ).astype(jnp.bfloat16)

    def encode(g):
        first = pl.multiple_of(g * columns, columns)
        theirs = asks & (g % 2 == 1)

        @pl.when(helps & (g % 2 == 1))
        def _():
            ask(g).wait_recv()
            reach = pl.ds(pl.multiple_of((1 + outward) * rows, rows), span)
            help_out[g // 2] = attend(
                help_q[g // 2], kv[g, 0, reach], kv[g, 1, reach], help_bias
            )
            give_back(g).start()

        @pl.when(jnp.logical_not(theirs))
        def _():
            enc_ref[:, pl.ds(first, columns)] = attend(
                q_buf[:, pl.ds(first, columns)],
                kv[g, 0, rows : rows + span],
                kv[g, 1, rows : rows + span],
                bias,
            )

        @pl.when(theirs)
        def _():
            give_back(g).wait_recv()
            enc_ref[:, pl.ds(first, columns)] = returned[g // 2]

        encoded = enc_ref[:, pl.ds(first, columns)]
        picked = jnp.dot(choose, encoded, preferred_element_type=jnp.float32)
        squared = picked * picked
        for h in range(SHARE):
            squares[...] += squared[:, h * HEAD_DIM : (h + 1) * HEAD_DIM]
        gained = picked * gain_ref[:, pl.ds(first, columns)]
        mine[g] = jnp.concatenate((gained[:, :half], gained[:, half:]), axis=0).astype(jnp.bfloat16)

    def share(g, s, source):
        return pltpu.make_async_remote_copy(
            src_ref=mine.at[g],
            dst_ref=mem.at[g % per, source],
            send_sem=mem_send.at[g, s],
            recv_sem=mem_recv.at[g % per, source],
            device_id={"tp": g // per, "seq": s},
            device_id_type=MESH,
        )

    def each_share(g, act):
        for step in range(1, n_seq):
            act(share(g, (seq + step) % n_seq, me))

        @pl.when(g // per != tp)
        def _():
            act(share(g, seq, me))

    def scale_to(step):
        return pltpu.make_async_remote_copy(
            src_ref=scales.at[seq],
            dst_ref=scales.at[seq],
            send_sem=scale_send.at[step],
            recv_sem=scale_recv.at[seq],
            device_id={"tp": tp, "seq": (seq + step) % n_seq},
            device_id_type=MESH,
        )

    def reduce(step):
        other = (tp + step) % n_tp
        return pltpu.make_async_remote_copy(
            src_ref=part.at[other],
            dst_ref=red.at[tp],
            send_sem=red_send.at[step],
            recv_sem=red_recv.at[tp],
            device_id={"tp": other, "seq": seq},
            device_id_type=MESH,
        )

    def project(g):
        place = g % per

        @pl.loop(1, n)
        def _(step):
            source = (me + step) % n
            share(per * tp + place, seq, source).wait_recv()

        gathered = mem[place].astype(jnp.float32)
        left = gathered[:, :picks].reshape(n * picks, half)
        right = gathered[:, picks:].reshape(n * picks, half)
        memory = jnp.concatenate((left, right), axis=1).astype(jnp.bfloat16)
        down_to = pl.multiple_of(place * columns, columns)
        for j in range(cols // tile):
            where = slice(j * tile, (j + 1) * tile)
            sums[:, where] += jnp.dot(
                memory, w_buf[pl.ds(down_to, columns), where], preferred_element_type=jnp.float32
            )

        @pl.when(place == per - 1)
        def _():
            part[...] = sums[...].reshape(n_tp, n_seq * picks, cols).astype(jnp.bfloat16)
            for step in range(1, n_tp):
                reduce(step).start()

    pl.semaphore_wait(barrier, n - 1)
    q_copy.wait()
    for c in range(AHEAD):
        own(c)
    w_copy.wait()

    @pl.loop(0, KV_HEADS + prior)
    def _(t):
        @pl.when(t + AHEAD < KV_HEADS)
        def _():
            own(t + AHEAD)

        for depth in range(1, prior + 1):
            c = t - (depth - 1)

            @pl.when((c >= 0) & (c < KV_HEADS))
            def _():
                from_below(c, depth)
                from_before(c, prior + 1 - depth)

        g = t - (prior - 1)

        @pl.when((g >= 0) & (g < KV_HEADS))
        def _():
            encode(g)
            each_share(g, lambda copy: copy.start())

            @pl.when(g // per == tp)
            def _():
                mem[g % per, me] = mine[g]

        @pl.when(g == KV_HEADS - 1)
        def _():
            meansq = jnp.sum(squares[...], axis=1, keepdims=True) / D
            scales[seq] = jnp.broadcast_to(lax.rsqrt(meansq + 1e-05), scales.shape[1:])
            for step in range(1, n_seq):
                scale_to(step).start()

        @pl.when((g >= 1) & ((g - 1) // per == tp))
        def _():
            project(g - 1)

    total = part[tp].astype(jnp.float32)
    for step in range(1, n_tp):
        source = (tp + step) % n_tp
        pltpu.make_async_remote_copy(
            src_ref=part.at[0],
            dst_ref=red.at[source],
            send_sem=red_send.at[step],
            recv_sem=red_recv.at[source],
            device_id={"tp": source, "seq": seq},
            device_id_type=MESH,
        ).wait_recv()
        total = total + red[source].astype(jnp.float32)
    for step in range(1, n_seq):
        source = (seq + step) % n_seq
        pltpu.make_async_remote_copy(
            src_ref=scales.at[source],
            dst_ref=scales.at[source],
            send_sem=scale_send.at[step],
            recv_sem=scale_recv.at[source],
            device_id={"tp": tp, "seq": source},
            device_id_type=MESH,
        ).wait_recv()
    factor = scales[...].reshape(n_seq * picks, HEAD_DIM)[:, :1]
    sum_ref[...] = (total * factor).astype(jnp.bfloat16)

    for step in range(1, n_tp):
        reduce(step).wait_send()
    for step in range(1, n_seq):
        scale_to(step).wait_send()

    @pl.loop(0, KV_HEADS)
    def _(g):
        each_share(g, lambda copy: copy.wait_send())

    @pl.loop(0, KV_HEADS)
    def _(c):
        each_own(c, lambda copy: copy.wait_send())

        for k in range(1, prior):

            @pl.when((seq >= k) & has_up(c))
            def _():
                up(c, k).wait_send()

        for k in range(2, prior + 1):

            @pl.when((seq < k) & (tp > 0) & has_down(c))
            def _():
                down(c, k).wait_send()

        @pl.when(is_bottom & (c % 2 == 1))
        def _():
            extra_up(c).wait_send()

        @pl.when(helps & (c % 2 == 1))
        def _():
            give_back(c).wait_send()


def on_device(n_tp, n_seq, queries, keys, values, mem_pos, norm_gain, summary_weight):
    rows = queries.shape[0]
    picks = mem_pos.shape[0]
    prior = -(-(WINDOW - 1) // rows)
    n = n_tp * n_seq
    width = summary_weight.shape[0]
    cols = summary_weight.shape[1]
    per = KV_HEADS // n_tp
    half = width // per // 2
    vmem = pl.BlockSpec(memory_space=pltpu.VMEM)
    anywhere = pl.BlockSpec(memory_space=pl.ANY)
    bf16 = jnp.bfloat16
    dma = pltpu.SemaphoreType.DMA
    span = (prior + 1) * rows
    results = pl.pallas_call(
        functools.partial(kernel, n_tp, n_seq, prior),
        out_shape=(
            jax.ShapeDtypeStruct((rows, D), bf16),
            jax.ShapeDtypeStruct((n_seq * picks, cols), bf16),
        ),
        in_specs=[
            anywhere, vmem, vmem, pl.BlockSpec(memory_space=pltpu.SMEM), vmem, anywhere,
        ],
        out_specs=(vmem, vmem),
        scratch_shapes=[
            pltpu.VMEM((rows, D), bf16),
            pltpu.VMEM((width, cols), bf16),
            pltpu.VMEM((KV_HEADS, 2, (prior + 3) * rows, HEAD_DIM), bf16),
            pltpu.VMEM((span, rows), jnp.float32),
            pltpu.VMEM((span, rows), jnp.float32),
            pltpu.VMEM((picks, HEAD_DIM), jnp.float32),
            pltpu.VMEM((KV_HEADS, 2 * picks, half), bf16),
            pltpu.VMEM((per, n, 2 * picks, half), bf16),
            pltpu.VMEM((n * picks, cols), jnp.float32),
            pltpu.VMEM((n_tp, n_seq * picks, cols), bf16),
            pltpu.VMEM((n_tp, n_seq * picks, cols), bf16),
            pltpu.VMEM((n_seq, picks, HEAD_DIM), jnp.float32),
            pltpu.VMEM((KV_HEADS // 2, rows, D // KV_HEADS), bf16),
            pltpu.VMEM((KV_HEADS // 2, rows, D // KV_HEADS), bf16),
            pltpu.VMEM((KV_HEADS // 2, rows, D // KV_HEADS), bf16),
            dma((2,)),
            dma((3, prior + 1, KV_HEADS)),
            dma((prior + 3, KV_HEADS)),
            dma((KV_HEADS, n_seq)),
            dma((per, n)),
            dma((n_tp,)),
            dma((n_tp,)),
            dma((n_seq,)),
            dma((n_seq,)),
            dma((KV_HEADS // 2,)),
            dma((KV_HEADS // 2,)),
            dma((KV_HEADS // 2,)),
            dma((KV_HEADS // 2,)),
        ],
        compiler_params=pltpu.CompilerParams(
            collective_id=0, has_side_effects=True, vmem_limit_bytes=60 * 1024 * 1024
        ),
        cost_estimate=pl.CostEstimate(
            flops=4 * HEADS * rows * span * HEAD_DIM + 2 * n * picks * width * cols,
            bytes_accessed=2 * (2 * rows * D + 4 * rows * KV_HEADS * HEAD_DIM + width * cols),
            transcendentals=HEADS * rows * span,
        ),
    )(queries, keys, values, mem_pos, norm_gain.reshape(1, D), summary_weight)
    return pl.pallas_call(
        hand_over,
        out_shape=tuple(jax.ShapeDtypeStruct(r.shape, r.dtype) for r in results),
        in_specs=[anywhere, anywhere],
        out_specs=(anywhere, anywhere),
        scratch_shapes=[
            *(pltpu.VMEM(r.shape, r.dtype) for r in results),
            dma((2, PIECES + 1)),
        ],
        compiler_params=pltpu.CompilerParams(vmem_limit_bytes=60 * 1024 * 1024),
    )(*results)


def solution(mesh):
    placed = (
        P(("file", "tp", "seq"), None),
        P(("file", "tp", "seq"), None),
        P(("file", "tp", "seq"), None),
        P(("file", "tp", "seq")),
        P(),
        P("tp", "seq"),
    )
    return jax.shard_map(
        functools.partial(on_device, mesh.shape["tp"], mesh.shape["seq"]),
        mesh=mesh,
        in_specs=placed,
        out_specs=(P(("file", "tp", "seq"), None), P(("file", "tp"), "seq")),
        check_vma=False,
    )
```

```python
import functools
import math

import jax
import jax.numpy as jnp
from jax import lax
from jax.experimental import pallas as pl
from jax.experimental.pallas import tpu as pltpu
from jax.sharding import PartitionSpec as P

D = 4096
HEADS = 32
KV_HEADS = 8
HEAD_DIM = 128
WINDOW = 512
SHARE = HEADS // KV_HEADS
MESH = pl.DeviceIdType.MESH
AHEAD = 4
LEAD = 2
LAG = 2
PIECES = 4


def hand_over(enc_from, sum_from, enc_to, sum_to, enc_buf, sum_buf, sems):
    rows = enc_from.shape[0] // PIECES
    parts = [(sum_from, sum_buf, sum_to)]
    for i in range(PIECES):
        piece = pl.ds(i * rows, rows)
        parts.append((enc_from.at[piece], enc_buf.at[piece], enc_to.at[piece]))
    into = [pltpu.make_async_copy(a, b, sems.at[0, i]) for i, (a, b, c) in enumerate(parts)]
    out = [pltpu.make_async_copy(b, c, sems.at[1, i]) for i, (a, b, c) in enumerate(parts)]
    for copy in into:
        copy.start()
    for first, second in zip(into, out):
        first.wait()
        second.start()
    for copy in out:
        copy.wait()


def kernel(
    n_tp, n_seq, prior,
    q_hbm, k_ref, v_ref, pos_ref, gain_ref, w_hbm,
    enc_ref, sum_ref,
    q_buf, w_buf, kv, bias, squares, mine, mem, sums, part, red, scales,
    local_sem, kv_send, kv_recv, mem_send, mem_recv, red_send, red_recv, scale_send, scale_recv,
):
    tp = lax.axis_index("tp")
    seq = lax.axis_index("seq")
    me = tp * n_seq + seq
    n = n_tp * n_seq
    rows = k_ref.shape[0]
    assert rows == HEAD_DIM
    span = (prior + 1) * rows
    picks = pos_ref.shape[0]
    per = KV_HEADS // n_tp
    columns = SHARE * HEAD_DIM
    half = columns // 2
    cols = sum_ref.shape[1]
    tile = 512 if cols % 512 == 0 else cols
    squares[...] = jnp.zeros_like(squares)
    sums[...] = jnp.zeros_like(sums)

    def device(index):
        return {"tp": index // n_seq, "seq": index % n_seq}

    q_copy = pltpu.make_async_copy(q_hbm, q_buf, local_sem.at[0])
    w_copy = pltpu.make_async_copy(w_hbm, w_buf, local_sem.at[1])
    q_copy.start()
    w_copy.start()

    barrier = pltpu.get_barrier_semaphore()

    @pl.loop(1, n)
    def _(step):
        pl.semaphore_signal(
            barrier, inc=1, device_id=device((me + step) % n), device_id_type=MESH
        )

    for g in range(KV_HEADS):
        kv[g, 0, prior * rows :, :] = k_ref[:, g * HEAD_DIM : (g + 1) * HEAD_DIM]
        kv[g, 1, prior * rows :, :] = v_ref[:, g * HEAD_DIM : (g + 1) * HEAD_DIM].T
    for k in range(1, prior + 1):

        @pl.when(me < k)
        def _():
            start = (prior - k) * rows
            kv[:, :, start : start + rows, :] = jnp.zeros(
                (KV_HEADS, 2, rows, HEAD_DIM), jnp.bfloat16
            )

    row = lax.broadcasted_iota(jnp.int32, (span, rows), 1)
    col = lax.broadcasted_iota(jnp.int32, (span, rows), 0) - prior * rows
    seen = (col <= row) & (col > row - WINDOW) & (col + me * rows >= 0)
    bias[...] = jnp.where(seen, 0.0, -jnp.inf).astype(jnp.float32)

    pick_row = lax.broadcasted_iota(jnp.int32, (picks, rows), 0)
    pick_col = lax.broadcasted_iota(jnp.int32, (picks, rows), 1)
    wanted = jnp.zeros((picks, rows), jnp.int32)
    for j in range(picks):
        wanted = jnp.where(pick_row == j, pos_ref[j] - me * rows, wanted)
    choose = jnp.where(pick_col == wanted, 1.0, 0.0).astype(jnp.bfloat16)

    def slot(c, k):
        return kv.at[c, :, pl.ds((prior - k) * rows, rows), :]

    def send(c, k, lands, target, way):
        return pltpu.make_async_remote_copy(
            src_ref=slot(c, k),
            dst_ref=slot(c, lands),
            send_sem=kv_send.at[way, c],
            recv_sem=kv_recv.at[lands, c],
            device_id=target,
            device_id_type=MESH,
        )

    def each_own(c, act):
        for k in range(1, prior + 1):
            direct = me + k < n
            if k == 1:
                direct = direct & (seq + 1 < n_seq)
            if k == 3:
                direct = direct & (seq + 3 >= n_seq)

            @pl.when(direct)
            def _():
                act(send(c, 0, k, device(me + k), k))

    def each_forward(c, act):
        @pl.when((seq >= 2) & (seq + 1 < n_seq))
        def _():
            act(send(c, 2, 3, device(me + 1), 0))

        @pl.when((seq == 1) & (tp > 0))
        def _():
            act(send(c, 2, 1, device(me - 1), 0))

    def arrive(c, k):
        @pl.when(me >= k)
        def _():
            send(c, 0, k, device(me), k).wait_recv()

    def own(c):
        each_own(c, lambda copy: copy.start())

    def forward(c):
        arrive(c, 2)
        each_forward(c, lambda copy: copy.start())

    fold = math.log2(math.e) / HEAD_DIM**0.5

    def attend(q_all, keys, flipped, bias):
        q_rows = jnp.concatenate(
            [q_all[:, h * HEAD_DIM : (h + 1) * HEAD_DIM] for h in range(SHARE)], axis=0
        )
        scores = lax.dot_general(
            keys, q_rows, (((1,), (1,)), ((), ())), preferred_element_type=jnp.float32
        )
        masked = scores + jnp.concatenate([bias[...]] * SHARE, axis=1)
        peak = jnp.max(masked, axis=0, keepdims=True)
        weights = jnp.exp2((masked - peak) * fold)
        total = jnp.sum(weights, axis=0, keepdims=True)
        values = jnp.concatenate(
            [flipped[b * rows : (b + 1) * rows] for b in range(prior + 1)], axis=1
        )
        mixed = jnp.dot(values, weights.astype(jnp.bfloat16), preferred_element_type=jnp.float32)
        mixed = mixed * (1.0 / total)
        return jnp.concatenate(
            [mixed[:, h * rows : (h + 1) * rows].T for h in range(SHARE)], axis=1
        ).astype(jnp.bfloat16)

    def encode(g):
        first = pl.multiple_of(g * columns, columns)
        encoded = attend(q_buf[:, pl.ds(first, columns)], kv[g, 0], kv[g, 1], bias)
        enc_ref[:, pl.ds(first, columns)] = encoded
        picked = jnp.dot(choose, encoded, preferred_element_type=jnp.float32)
        squared = picked * picked
        for h in range(SHARE):
            squares[...] += squared[:, h * HEAD_DIM : (h + 1) * HEAD_DIM]
        gained = picked * gain_ref[:, pl.ds(first, columns)]
        mine[g] = jnp.concatenate((gained[:, :half], gained[:, half:]), axis=0).astype(jnp.bfloat16)

    def share(g, s, source):
        return pltpu.make_async_remote_copy(
            src_ref=mine.at[g],
            dst_ref=mem.at[g % per, source],
            send_sem=mem_send.at[g, s],
            recv_sem=mem_recv.at[g % per, source],
            device_id={"tp": g // per, "seq": s},
            device_id_type=MESH,
        )

    def each_share(g, act):
        for step in range(1, n_seq):
            act(share(g, (seq + step) % n_seq, me))

        @pl.when(g // per != tp)
        def _():
            act(share(g, seq, me))

    def scale_to(step):
        return pltpu.make_async_remote_copy(
            src_ref=scales.at[seq],
            dst_ref=scales.at[seq],
            send_sem=scale_send.at[step],
            recv_sem=scale_recv.at[seq],
            device_id={"tp": tp, "seq": (seq + step) % n_seq},
            device_id_type=MESH,
        )

    def reduce(step):
        other = (tp + step) % n_tp
        return pltpu.make_async_remote_copy(
            src_ref=part.at[other],
            dst_ref=red.at[tp],
            send_sem=red_send.at[step],
            recv_sem=red_recv.at[tp],
            device_id={"tp": other, "seq": seq},
            device_id_type=MESH,
        )

    def project(g):
        place = g % per

        @pl.loop(1, n)
        def _(step):
            source = (me + step) % n
            share(per * tp + place, seq, source).wait_recv()

        gathered = mem[place].astype(jnp.float32)
        left = gathered[:, :picks].reshape(n * picks, half)
        right = gathered[:, picks:].reshape(n * picks, half)
        memory = jnp.concatenate((left, right), axis=1).astype(jnp.bfloat16)
        down_to = pl.multiple_of(place * columns, columns)
        for j in range(cols // tile):
            where = slice(j * tile, (j + 1) * tile)
            sums[:, where] += jnp.dot(
                memory, w_buf[pl.ds(down_to, columns), where], preferred_element_type=jnp.float32
            )

        @pl.when(place == per - 1)
        def _():
            part[...] = sums[...].reshape(n_tp, n_seq * picks, cols).astype(jnp.bfloat16)
            for step in range(1, n_tp):
                reduce(step).start()

    pl.semaphore_wait(barrier, n - 1)
    for c in range(AHEAD):
        own(c)
    for c in range(LEAD):
        forward(c)
    q_copy.wait()
    w_copy.wait()

    @pl.loop(0, KV_HEADS + LAG)
    def _(g):
        @pl.when(g + AHEAD < KV_HEADS)
        def _():
            own(g + AHEAD)

        @pl.when(g + LEAD < KV_HEADS)
        def _():
            forward(g + LEAD)

        @pl.when(g < KV_HEADS)
        def _():
            for k in range(1, prior + 1):
                if k != 2:
                    arrive(g, k)
            encode(g)
            each_share(g, lambda copy: copy.start())

            @pl.when(g // per == tp)
            def _():
                mem[g % per, me] = mine[g]

        @pl.when(g == KV_HEADS - 1)
        def _():
            meansq = jnp.sum(squares[...], axis=1, keepdims=True) / D
            scales[seq] = jnp.broadcast_to(lax.rsqrt(meansq + 1e-05), scales.shape[1:])
            for step in range(1, n_seq):
                scale_to(step).start()

        @pl.when((g >= LAG) & ((g - LAG) // per == tp))
        def _():
            project(g - LAG)

    total = part[tp].astype(jnp.float32)
    for step in range(1, n_tp):
        source = (tp + step) % n_tp
        pltpu.make_async_remote_copy(
            src_ref=part.at[0],
            dst_ref=red.at[source],
            send_sem=red_send.at[step],
            recv_sem=red_recv.at[source],
            device_id={"tp": source, "seq": seq},
            device_id_type=MESH,
        ).wait_recv()
        total = total + red[source].astype(jnp.float32)
    for step in range(1, n_seq):
        source = (seq + step) % n_seq
        pltpu.make_async_remote_copy(
            src_ref=scales.at[source],
            dst_ref=scales.at[source],
            send_sem=scale_send.at[step],
            recv_sem=scale_recv.at[source],
            device_id={"tp": tp, "seq": source},
            device_id_type=MESH,
        ).wait_recv()
    factor = scales[...].reshape(n_seq * picks, HEAD_DIM)[:, :1]
    sum_ref[...] = (total * factor).astype(jnp.bfloat16)

    for step in range(1, n_tp):
        reduce(step).wait_send()
    for step in range(1, n_seq):
        scale_to(step).wait_send()

    @pl.loop(0, KV_HEADS)
    def _(g):
        each_share(g, lambda copy: copy.wait_send())

    @pl.loop(0, KV_HEADS)
    def _(c):
        each_own(c, lambda copy: copy.wait_send())
        each_forward(c, lambda copy: copy.wait_send())


def on_device(n_tp, n_seq, queries, keys, values, mem_pos, norm_gain, summary_weight):
    rows = queries.shape[0]
    picks = mem_pos.shape[0]
    prior = -(-(WINDOW - 1) // rows)
    n = n_tp * n_seq
    width = summary_weight.shape[0]
    cols = summary_weight.shape[1]
    per = KV_HEADS // n_tp
    half = width // per // 2
    vmem = pl.BlockSpec(memory_space=pltpu.VMEM)
    anywhere = pl.BlockSpec(memory_space=pl.ANY)
    bf16 = jnp.bfloat16
    dma = pltpu.SemaphoreType.DMA
    span = (prior + 1) * rows
    results = pl.pallas_call(
        functools.partial(kernel, n_tp, n_seq, prior),
        out_shape=(
            jax.ShapeDtypeStruct((rows, D), bf16),
            jax.ShapeDtypeStruct((n_seq * picks, cols), bf16),
        ),
        in_specs=[
            anywhere, vmem, vmem, pl.BlockSpec(memory_space=pltpu.SMEM), vmem, anywhere,
        ],
        out_specs=(vmem, vmem),
        scratch_shapes=[
            pltpu.VMEM((rows, D), bf16),
            pltpu.VMEM((width, cols), bf16),
            pltpu.VMEM((KV_HEADS, 2, span, HEAD_DIM), bf16),
            pltpu.VMEM((span, rows), jnp.float32),
            pltpu.VMEM((picks, HEAD_DIM), jnp.float32),
            pltpu.VMEM((KV_HEADS, 2 * picks, half), bf16),
            pltpu.VMEM((per, n, 2 * picks, half), bf16),
            pltpu.VMEM((n * picks, cols), jnp.float32),
            pltpu.VMEM((n_tp, n_seq * picks, cols), bf16),
            pltpu.VMEM((n_tp, n_seq * picks, cols), bf16),
            pltpu.VMEM((n_seq, picks, HEAD_DIM), jnp.float32),
            dma((2,)),
            dma((prior + 1, KV_HEADS)),
            dma((prior + 1, KV_HEADS)),
            dma((KV_HEADS, n_seq)),
            dma((per, n)),
            dma((n_tp,)),
            dma((n_tp,)),
            dma((n_seq,)),
            dma((n_seq,)),
        ],
        compiler_params=pltpu.CompilerParams(
            collective_id=0, has_side_effects=True, vmem_limit_bytes=60 * 1024 * 1024
        ),
        cost_estimate=pl.CostEstimate(
            flops=4 * HEADS * rows * span * HEAD_DIM + 2 * n * picks * width * cols,
            bytes_accessed=2 * (2 * rows * D + 4 * rows * KV_HEADS * HEAD_DIM + width * cols),
            transcendentals=HEADS * rows * span,
        ),
    )(queries, keys, values, mem_pos, norm_gain.reshape(1, D), summary_weight)
    return pl.pallas_call(
        hand_over,
        out_shape=tuple(jax.ShapeDtypeStruct(r.shape, r.dtype) for r in results),
        in_specs=[anywhere, anywhere],
        out_specs=(anywhere, anywhere),
        scratch_shapes=[
            *(pltpu.VMEM(r.shape, r.dtype) for r in results),
            dma((2, PIECES + 1)),
        ],
        compiler_params=pltpu.CompilerParams(vmem_limit_bytes=60 * 1024 * 1024),
    )(*results)


def solution(mesh):
    placed = (
        P(("file", "tp", "seq"), None),
        P(("file", "tp", "seq"), None),
        P(("file", "tp", "seq"), None),
        P(("file", "tp", "seq")),
        P(),
        P("tp", "seq"),
    )
    return jax.shard_map(
        functools.partial(on_device, mesh.shape["tp"], mesh.shape["seq"]),
        mesh=mesh,
        in_specs=placed,
        out_specs=(P(("file", "tp", "seq"), None), P(("file", "tp"), "seq")),
        check_vma=False,
    )
```

```python
import functools
import math

import jax
import jax.numpy as jnp
from jax import lax
from jax.experimental import pallas as pl
from jax.experimental.pallas import tpu as pltpu
from jax.sharding import PartitionSpec as P

D = 4096
HEADS = 32
KV_HEADS = 8
HEAD_DIM = 128
WINDOW = 512
SHARE = HEADS // KV_HEADS
MESH = pl.DeviceIdType.MESH
AHEAD = 2
LEAD = 1
LAG = 1
PIECES = 4


def hand_over(enc_from, sum_from, enc_to, sum_to, enc_buf, sum_buf, sems):
    rows = enc_from.shape[0] // PIECES
    parts = [(sum_from, sum_buf, sum_to)]
    for i in range(PIECES):
        piece = pl.ds(i * rows, rows)
        parts.append((enc_from.at[piece], enc_buf.at[piece], enc_to.at[piece]))
    into = [pltpu.make_async_copy(a, b, sems.at[0, i]) for i, (a, b, c) in enumerate(parts)]
    out = [pltpu.make_async_copy(b, c, sems.at[1, i]) for i, (a, b, c) in enumerate(parts)]
    for copy in into:
        copy.start()
    for first, second in zip(into, out):
        first.wait()
        second.start()
    for copy in out:
        copy.wait()


def kernel(
    n_tp, n_seq, prior,
    q_hbm, k_ref, v_ref, pos_ref, gain_ref, w_hbm,
    enc_ref, sum_ref,
    q_buf, w_buf, kv, bias, squares, mine, mem, part, red, scales,
    local_sem, kv_send, kv_recv, mem_send, mem_recv, red_send, red_recv, scale_send, scale_recv,
):
    tp = lax.axis_index("tp")
    seq = lax.axis_index("seq")
    me = tp * n_seq + seq
    n = n_tp * n_seq
    rows = k_ref.shape[0]
    assert rows == HEAD_DIM
    span = (prior + 1) * rows
    picks = pos_ref.shape[0]
    per = KV_HEADS // n_tp
    columns = SHARE * HEAD_DIM
    chunks = KV_HEADS // per
    cols = sum_ref.shape[1]
    tile = 512 if cols % 512 == 0 else cols
    squares[...] = jnp.zeros_like(squares)

    def device(index):
        return {"tp": index // n_seq, "seq": index % n_seq}

    q_copy = pltpu.make_async_copy(q_hbm, q_buf, local_sem.at[0])
    w_copy = pltpu.make_async_copy(w_hbm, w_buf, local_sem.at[1])
    q_copy.start()
    w_copy.start()

    barrier = pltpu.get_barrier_semaphore()

    @pl.loop(1, n)
    def _(step):
        pl.semaphore_signal(
            barrier, inc=1, device_id=device((me + step) % n), device_id_type=MESH
        )

    for g in range(KV_HEADS):
        kv[g, 0, prior * rows :, :] = k_ref[:, g * HEAD_DIM : (g + 1) * HEAD_DIM]
        kv[g, 1, prior * rows :, :] = v_ref[:, g * HEAD_DIM : (g + 1) * HEAD_DIM].T
    for k in range(1, prior + 1):

        @pl.when(me < k)
        def _():
            start = (prior - k) * rows
            kv[:, :, start : start + rows, :] = jnp.zeros(
                (KV_HEADS, 2, rows, HEAD_DIM), jnp.bfloat16
            )

    row = lax.broadcasted_iota(jnp.int32, (span, rows), 1)
    col = lax.broadcasted_iota(jnp.int32, (span, rows), 0) - prior * rows
    seen = (col <= row) & (col > row - WINDOW) & (col + me * rows >= 0)
    bias[...] = jnp.where(seen, 0.0, -jnp.inf).astype(jnp.float32)

    pick_row = lax.broadcasted_iota(jnp.int32, (picks, rows), 0)
    pick_col = lax.broadcasted_iota(jnp.int32, (picks, rows), 1)
    wanted = jnp.zeros((picks, rows), jnp.int32)
    for j in range(picks):
        wanted = jnp.where(pick_row == j, pos_ref[j] - me * rows, wanted)
    choose = jnp.where(pick_col == wanted, 1.0, 0.0).astype(jnp.bfloat16)

    def slot(c, k):
        return kv.at[pl.ds(c * per, per), :, pl.ds((prior - k) * rows, rows), :]

    def send(c, k, lands, target, way):
        return pltpu.make_async_remote_copy(
            src_ref=slot(c, k),
            dst_ref=slot(c, lands),
            send_sem=kv_send.at[way, c],
            recv_sem=kv_recv.at[lands, c],
            device_id=target,
            device_id_type=MESH,
        )

    def each_own(c, act):
        for k in range(1, prior + 1):
            direct = me + k < n
            if k == 1:
                direct = direct & (seq + 1 < n_seq)
            if k == 3:
                direct = direct & (seq + 3 >= n_seq)

            @pl.when(direct)
            def _():
                act(send(c, 0, k, device(me + k), k))

    def each_forward(c, act):
        @pl.when((seq >= 2) & (seq + 1 < n_seq))
        def _():
            act(send(c, 2, 3, device(me + 1), 0))

        @pl.when((seq == 1) & (tp > 0))
        def _():
            act(send(c, 2, 1, device(me - 1), 0))

    def arrive(c, k):
        @pl.when(me >= k)
        def _():
            send(c, 0, k, device(me), k).wait_recv()

    def own(c):
        each_own(c, lambda copy: copy.start())

    def forward(c):
        arrive(c, 2)
        each_forward(c, lambda copy: copy.start())

    fold = math.log2(math.e) / HEAD_DIM**0.5

    def attend(q_all, keys, flipped, bias):
        q_rows = jnp.concatenate(
            [q_all[:, h * HEAD_DIM : (h + 1) * HEAD_DIM] for h in range(SHARE)], axis=0
        )
        scores = lax.dot_general(
            keys, q_rows, (((1,), (1,)), ((), ())), preferred_element_type=jnp.float32
        )
        masked = scores + jnp.concatenate([bias[...]] * SHARE, axis=1)
        peak = jnp.max(masked, axis=0, keepdims=True)
        weights = jnp.exp2((masked - peak) * fold)
        total = jnp.sum(weights, axis=0, keepdims=True)
        values = jnp.concatenate(
            [flipped[b * rows : (b + 1) * rows] for b in range(prior + 1)], axis=1
        )
        mixed = jnp.dot(values, weights.astype(jnp.bfloat16), preferred_element_type=jnp.float32)
        mixed = mixed * (1.0 / total)
        return jnp.concatenate(
            [mixed[:, h * rows : (h + 1) * rows].T for h in range(SHARE)], axis=1
        ).astype(jnp.bfloat16)

    def encode(c):
        gained = []
        for j in range(per):
            g = c * per + j
            first = pl.multiple_of(g * columns, columns)
            encoded = attend(q_buf[:, pl.ds(first, columns)], kv[g, 0], kv[g, 1], bias)
            enc_ref[:, pl.ds(first, columns)] = encoded
            picked = jnp.dot(choose, encoded, preferred_element_type=jnp.float32)
            squared = picked * picked
            for h in range(SHARE):
                squares[...] += squared[:, h * HEAD_DIM : (h + 1) * HEAD_DIM]
            gained.append(picked * gain_ref[:, pl.ds(first, columns)])
        mine[c] = jnp.concatenate(gained, axis=0).astype(jnp.bfloat16)

    def share(c, s, source):
        return pltpu.make_async_remote_copy(
            src_ref=mine.at[c],
            dst_ref=mem.at[source],
            send_sem=mem_send.at[c, s],
            recv_sem=mem_recv.at[source],
            device_id={"tp": c, "seq": s},
            device_id_type=MESH,
        )

    def each_share(c, act):
        for step in range(1, n_seq):
            act(share(c, (seq + step) % n_seq, me))

        @pl.when(c != tp)
        def _():
            act(share(c, seq, me))

    def scale_to(step):
        return pltpu.make_async_remote_copy(
            src_ref=scales.at[seq],
            dst_ref=scales.at[seq],
            send_sem=scale_send.at[step],
            recv_sem=scale_recv.at[seq],
            device_id={"tp": tp, "seq": (seq + step) % n_seq},
            device_id_type=MESH,
        )

    def reduce(step):
        other = (tp + step) % n_tp
        return pltpu.make_async_remote_copy(
            src_ref=part.at[other],
            dst_ref=red.at[tp],
            send_sem=red_send.at[step],
            recv_sem=red_recv.at[tp],
            device_id={"tp": other, "seq": seq},
            device_id_type=MESH,
        )

    def project():
        @pl.loop(1, n)
        def _(step):
            source = (me + step) % n
            share(tp, seq, source).wait_recv()

        gathered = mem[...].astype(jnp.float32)
        memory = jnp.concatenate(
            [
                gathered[:, j * picks : (j + 1) * picks].reshape(n * picks, columns)
                for j in range(per)
            ],
            axis=1,
        ).astype(jnp.bfloat16)
        for j in range(cols // tile):
            where = slice(j * tile, (j + 1) * tile)
            sums = jnp.dot(memory, w_buf[:, where], preferred_element_type=jnp.float32)
            part[:, :, where] = sums.reshape(n_tp, n_seq * picks, tile).astype(jnp.bfloat16)
        for step in range(1, n_tp):
            reduce(step).start()

    pl.semaphore_wait(barrier, n - 1)
    for c in range(AHEAD):
        own(c)
    for c in range(LEAD):
        forward(c)
    q_copy.wait()
    w_copy.wait()

    @pl.loop(0, chunks + LAG)
    def _(g):
        @pl.when(g + AHEAD < chunks)
        def _():
            own(g + AHEAD)

        @pl.when(g + LEAD < chunks)
        def _():
            forward(g + LEAD)

        @pl.when(g < chunks)
        def _():
            for k in range(1, prior + 1):
                if k != 2:
                    arrive(g, k)
            encode(g)
            each_share(g, lambda copy: copy.start())

            @pl.when(g == tp)
            def _():
                mem[me] = mine[g]

        @pl.when(g == chunks - 1)
        def _():
            meansq = jnp.sum(squares[...], axis=1, keepdims=True) / D
            scales[seq] = jnp.broadcast_to(lax.rsqrt(meansq + 1e-05), scales.shape[1:])
            for step in range(1, n_seq):
                scale_to(step).start()

        @pl.when(g - LAG == tp)
        def _():
            project()

    @pl.loop(0, chunks)
    def _(c):
        each_share(c, lambda copy: copy.wait_send())
        each_own(c, lambda copy: copy.wait_send())
        each_forward(c, lambda copy: copy.wait_send())

    total = part[tp].astype(jnp.float32)
    for step in range(1, n_tp):
        source = (tp + step) % n_tp
        pltpu.make_async_remote_copy(
            src_ref=part.at[0],
            dst_ref=red.at[source],
            send_sem=red_send.at[step],
            recv_sem=red_recv.at[source],
            device_id={"tp": source, "seq": seq},
            device_id_type=MESH,
        ).wait_recv()
        total = total + red[source].astype(jnp.float32)
    for step in range(1, n_seq):
        source = (seq + step) % n_seq
        pltpu.make_async_remote_copy(
            src_ref=scales.at[source],
            dst_ref=scales.at[source],
            send_sem=scale_send.at[step],
            recv_sem=scale_recv.at[source],
            device_id={"tp": tp, "seq": source},
            device_id_type=MESH,
        ).wait_recv()
    factor = scales[...].reshape(n_seq * picks, HEAD_DIM)[:, :1]
    sum_ref[...] = (total * factor).astype(jnp.bfloat16)

    for step in range(1, n_tp):
        reduce(step).wait_send()
    for step in range(1, n_seq):
        scale_to(step).wait_send()


def on_device(n_tp, n_seq, queries, keys, values, mem_pos, norm_gain, summary_weight):
    rows = queries.shape[0]
    picks = mem_pos.shape[0]
    prior = -(-(WINDOW - 1) // rows)
    n = n_tp * n_seq
    width = summary_weight.shape[0]
    cols = summary_weight.shape[1]
    per = KV_HEADS // n_tp
    chunks = KV_HEADS // per
    columns = width // per
    vmem = pl.BlockSpec(memory_space=pltpu.VMEM)
    anywhere = pl.BlockSpec(memory_space=pl.ANY)
    bf16 = jnp.bfloat16
    dma = pltpu.SemaphoreType.DMA
    span = (prior + 1) * rows
    results = pl.pallas_call(
        functools.partial(kernel, n_tp, n_seq, prior),
        out_shape=(
            jax.ShapeDtypeStruct((rows, D), bf16),
            jax.ShapeDtypeStruct((n_seq * picks, cols), bf16),
        ),
        in_specs=[
            anywhere, vmem, vmem, pl.BlockSpec(memory_space=pltpu.SMEM), vmem, anywhere,
        ],
        out_specs=(vmem, vmem),
        scratch_shapes=[
            pltpu.VMEM((rows, D), bf16),
            pltpu.VMEM((width, cols), bf16),
            pltpu.VMEM((KV_HEADS, 2, span, HEAD_DIM), bf16),
            pltpu.VMEM((span, rows), jnp.float32),
            pltpu.VMEM((picks, HEAD_DIM), jnp.float32),
            pltpu.VMEM((chunks, per * picks, columns), bf16),
            pltpu.VMEM((n, per * picks, columns), bf16),
            pltpu.VMEM((n_tp, n_seq * picks, cols), bf16),
            pltpu.VMEM((n_tp, n_seq * picks, cols), bf16),
            pltpu.VMEM((n_seq, picks, HEAD_DIM), jnp.float32),
            dma((2,)),
            dma((prior + 1, chunks)),
            dma((prior + 1, chunks)),
            dma((chunks, n_seq)),
            dma((n,)),
            dma((n_tp,)),
            dma((n_tp,)),
            dma((n_seq,)),
            dma((n_seq,)),
        ],
        compiler_params=pltpu.CompilerParams(
            collective_id=0, has_side_effects=True, vmem_limit_bytes=60 * 1024 * 1024
        ),
        cost_estimate=pl.CostEstimate(
            flops=4 * HEADS * rows * span * HEAD_DIM + 2 * n * picks * width * cols,
            bytes_accessed=2 * (2 * rows * D + 4 * rows * KV_HEADS * HEAD_DIM + width * cols),
            transcendentals=HEADS * rows * span,
        ),
    )(queries, keys, values, mem_pos, norm_gain.reshape(1, D), summary_weight)
    return pl.pallas_call(
        hand_over,
        out_shape=tuple(jax.ShapeDtypeStruct(r.shape, r.dtype) for r in results),
        in_specs=[anywhere, anywhere],
        out_specs=(anywhere, anywhere),
        scratch_shapes=[
            *(pltpu.VMEM(r.shape, r.dtype) for r in results),
            dma((2, PIECES + 1)),
        ],
        compiler_params=pltpu.CompilerParams(vmem_limit_bytes=60 * 1024 * 1024),
    )(*results)


def solution(mesh):
    placed = (
        P(("file", "tp", "seq"), None),
        P(("file", "tp", "seq"), None),
        P(("file", "tp", "seq"), None),
        P(("file", "tp", "seq")),
        P(),
        P("tp", "seq"),
    )
    return jax.shard_map(
        functools.partial(on_device, mesh.shape["tp"], mesh.shape["seq"]),
        mesh=mesh,
        in_specs=placed,
        out_specs=(P(("file", "tp", "seq"), None), P(("file", "tp"), "seq")),
        check_vma=False,
    )
```

```python
import functools
import math

import jax
import jax.numpy as jnp
from jax import lax
from jax.experimental import pallas as pl
from jax.experimental.pallas import tpu as pltpu
from jax.sharding import PartitionSpec as P

D = 4096
HEADS = 32
KV_HEADS = 8
HEAD_DIM = 128
WINDOW = 512
SHARE = HEADS // KV_HEADS
MESH = pl.DeviceIdType.MESH
AHEAD = 2
LEAD = 1
LAG = 1
PIECES = 4


def hand_over(enc_from, sum_from, enc_to, sum_to, enc_buf, sum_buf, sems):
    rows = enc_from.shape[0] // PIECES
    parts = [(sum_from, sum_buf, sum_to)]
    for i in range(PIECES):
        piece = pl.ds(i * rows, rows)
        parts.append((enc_from.at[piece], enc_buf.at[piece], enc_to.at[piece]))
    into = [pltpu.make_async_copy(a, b, sems.at[0, i]) for i, (a, b, c) in enumerate(parts)]
    out = [pltpu.make_async_copy(b, c, sems.at[1, i]) for i, (a, b, c) in enumerate(parts)]
    for copy in into:
        copy.start()
    for first, second in zip(into, out):
        first.wait()
        second.start()
    for copy in out:
        copy.wait()


def kernel(
    n_tp, n_seq, prior,
    q_hbm, k_ref, v_ref, pos_ref, gain_ref, w_hbm,
    enc_ref, sum_ref,
    q_buf, w_buf, kv, bias, squares, mine, mem, part, red, scales, enc_buf, enc_sem,
    local_sem, kv_send, kv_recv, mem_send, mem_recv, red_send, red_recv, scale_send, scale_recv,
):
    tp = lax.axis_index("tp")
    seq = lax.axis_index("seq")
    me = tp * n_seq + seq
    n = n_tp * n_seq
    rows = k_ref.shape[0]
    assert rows == HEAD_DIM
    span = (prior + 1) * rows
    picks = pos_ref.shape[0]
    per = KV_HEADS // n_tp
    columns = SHARE * HEAD_DIM
    chunks = KV_HEADS // per
    cols = sum_ref.shape[1]
    tile = 512 if cols % 512 == 0 else cols
    squares[...] = jnp.zeros_like(squares)

    def device(index):
        return {"tp": index // n_seq, "seq": index % n_seq}

    q_copy = pltpu.make_async_copy(q_hbm, q_buf, local_sem.at[0])
    w_copy = pltpu.make_async_copy(w_hbm, w_buf, local_sem.at[1])
    q_copy.start()
    w_copy.start()

    barrier = pltpu.get_barrier_semaphore()

    @pl.loop(1, n)
    def _(step):
        pl.semaphore_signal(
            barrier, inc=1, device_id=device((me + step) % n), device_id_type=MESH
        )

    for g in range(KV_HEADS):
        kv[g, 0, prior * rows :, :] = k_ref[:, g * HEAD_DIM : (g + 1) * HEAD_DIM]
        kv[g, 1, prior * rows :, :] = v_ref[:, g * HEAD_DIM : (g + 1) * HEAD_DIM].T
    for k in range(1, prior + 1):

        @pl.when(me < k)
        def _():
            start = (prior - k) * rows
            kv[:, :, start : start + rows, :] = jnp.zeros(
                (KV_HEADS, 2, rows, HEAD_DIM), jnp.bfloat16
            )

    row = lax.broadcasted_iota(jnp.int32, (span, rows), 1)
    col = lax.broadcasted_iota(jnp.int32, (span, rows), 0) - prior * rows
    seen = (col <= row) & (col > row - WINDOW) & (col + me * rows >= 0)
    bias[...] = jnp.where(seen, 0.0, -jnp.inf).astype(jnp.float32)

    pick_row = lax.broadcasted_iota(jnp.int32, (picks, rows), 0)
    pick_col = lax.broadcasted_iota(jnp.int32, (picks, rows), 1)
    wanted = jnp.zeros((picks, rows), jnp.int32)
    for j in range(picks):
        wanted = jnp.where(pick_row == j, pos_ref[j] - me * rows, wanted)
    choose = jnp.where(pick_col == wanted, 1.0, 0.0).astype(jnp.bfloat16)

    def slot(c, k):
        return kv.at[pl.ds(c * per, per), :, pl.ds((prior - k) * rows, rows), :]

    def send(c, k, lands, target, way):
        return pltpu.make_async_remote_copy(
            src_ref=slot(c, k),
            dst_ref=slot(c, lands),
            send_sem=kv_send.at[way, c],
            recv_sem=kv_recv.at[lands, c],
            device_id=target,
            device_id_type=MESH,
        )

    def each_own(c, act):
        for k in range(1, prior + 1):
            direct = me + k < n
            if k == 1:
                direct = direct & (seq + 1 < n_seq)
            if k == 3:
                direct = direct & (seq + 3 >= n_seq)

            @pl.when(direct)
            def _():
                act(send(c, 0, k, device(me + k), k))

    def each_forward(c, act):
        @pl.when((seq >= 2) & (seq + 1 < n_seq))
        def _():
            act(send(c, 2, 3, device(me + 1), 0))

        @pl.when((seq == 1) & (tp > 0))
        def _():
            act(send(c, 2, 1, device(me - 1), 0))

    def arrive(c, k):
        @pl.when(me >= k)
        def _():
            send(c, 0, k, device(me), k).wait_recv()

    def own(c):
        each_own(c, lambda copy: copy.start())

    def forward(c):
        arrive(c, 2)
        each_forward(c, lambda copy: copy.start())

    fold = math.log2(math.e) / HEAD_DIM**0.5

    def attend(q_all, keys, flipped, bias):
        q_rows = jnp.concatenate(
            [q_all[:, h * HEAD_DIM : (h + 1) * HEAD_DIM] for h in range(SHARE)], axis=0
        )
        scores = lax.dot_general(
            keys, q_rows, (((1,), (1,)), ((), ())), preferred_element_type=jnp.float32
        )
        masked = scores + jnp.concatenate([bias[...]] * SHARE, axis=1)
        peak = jnp.max(masked, axis=0, keepdims=True)
        weights = jnp.exp2((masked - peak) * fold)
        total = jnp.sum(weights, axis=0, keepdims=True)
        values = jnp.concatenate(
            [flipped[b * rows : (b + 1) * rows] for b in range(prior + 1)], axis=1
        )
        mixed = jnp.dot(values, weights.astype(jnp.bfloat16), preferred_element_type=jnp.float32)
        mixed = mixed * (1.0 / total)
        return jnp.concatenate(
            [mixed[:, h * rows : (h + 1) * rows].T for h in range(SHARE)], axis=1
        ).astype(jnp.bfloat16)

    def encode(c):
        gained = []
        for j in range(per):
            g = c * per + j
            first = pl.multiple_of(g * columns, columns)
            encoded = attend(q_buf[:, pl.ds(first, columns)], kv[g, 0], kv[g, 1], bias)
            enc_buf[:, pl.ds(first, columns)] = encoded
            picked = jnp.dot(choose, encoded, preferred_element_type=jnp.float32)
            squared = picked * picked
            for h in range(SHARE):
                squares[...] += squared[:, h * HEAD_DIM : (h + 1) * HEAD_DIM]
            gained.append(picked * gain_ref[:, pl.ds(first, columns)])
        mine[c] = jnp.concatenate(gained, axis=0).astype(jnp.bfloat16)

    def write(c):
        where = pl.ds(pl.multiple_of(c * per * columns, columns), per * columns)
        return pltpu.make_async_copy(enc_buf.at[:, where], enc_ref.at[:, where], enc_sem.at[c])

    def share(c, s, source):
        return pltpu.make_async_remote_copy(
            src_ref=mine.at[c],
            dst_ref=mem.at[source],
            send_sem=mem_send.at[c, s],
            recv_sem=mem_recv.at[source],
            device_id={"tp": c, "seq": s},
            device_id_type=MESH,
        )

    def each_share(c, act):
        for step in range(1, n_seq):
            act(share(c, (seq + step) % n_seq, me))

        @pl.when(c != tp)
        def _():
            act(share(c, seq, me))

    def scale_to(step):
        return pltpu.make_async_remote_copy(
            src_ref=scales.at[seq],
            dst_ref=scales.at[seq],
            send_sem=scale_send.at[step],
            recv_sem=scale_recv.at[seq],
            device_id={"tp": tp, "seq": (seq + step) % n_seq},
            device_id_type=MESH,
        )

    def reduce(step, j):
        other = (tp + step) % n_tp
        return pltpu.make_async_remote_copy(
            src_ref=part.at[j, other],
            dst_ref=red.at[j, tp],
            send_sem=red_send.at[step, j],
            recv_sem=red_recv.at[tp, j],
            device_id={"tp": other, "seq": seq},
            device_id_type=MESH,
        )

    def project():
        @pl.loop(1, n)
        def _(step):
            source = (me + step) % n
            share(tp, seq, source).wait_recv()

        gathered = mem[...].astype(jnp.float32)
        memory = jnp.concatenate(
            [
                gathered[:, j * picks : (j + 1) * picks].reshape(n * picks, columns)
                for j in range(per)
            ],
            axis=1,
        ).astype(jnp.bfloat16)
        for j in range(cols // tile):
            where = slice(j * tile, (j + 1) * tile)
            sums = jnp.dot(memory, w_buf[:, where], preferred_element_type=jnp.float32)
            part[j] = sums.reshape(n_tp, n_seq * picks, tile).astype(jnp.bfloat16)
            for step in range(1, n_tp):
                reduce(step, j).start()

    pl.semaphore_wait(barrier, n - 1)
    for c in range(AHEAD):
        own(c)
    for c in range(LEAD):
        forward(c)
    q_copy.wait()
    w_copy.wait()

    @pl.loop(0, chunks + LAG)
    def _(g):
        @pl.when(g + AHEAD < chunks)
        def _():
            own(g + AHEAD)

        @pl.when(g + LEAD < chunks)
        def _():
            forward(g + LEAD)

        @pl.when(g < chunks)
        def _():
            for k in range(1, prior + 1):
                if k != 2:
                    arrive(g, k)
            encode(g)
            each_share(g, lambda copy: copy.start())
            write(g).start()

            @pl.when(g == tp)
            def _():
                mem[me] = mine[g]

        @pl.when(g == chunks - 1)
        def _():
            meansq = jnp.sum(squares[...], axis=1, keepdims=True) / D
            scales[seq] = jnp.broadcast_to(lax.rsqrt(meansq + 1e-05), scales.shape[1:])
            for step in range(1, n_seq):
                scale_to(step).start()

        @pl.when(g - LAG == tp)
        def _():
            project()

    @pl.loop(0, chunks)
    def _(c):
        write(c).wait()
        each_share(c, lambda copy: copy.wait_send())
        each_own(c, lambda copy: copy.wait_send())
        each_forward(c, lambda copy: copy.wait_send())

    for step in range(1, n_seq):
        source = (seq + step) % n_seq
        pltpu.make_async_remote_copy(
            src_ref=scales.at[source],
            dst_ref=scales.at[source],
            send_sem=scale_send.at[step],
            recv_sem=scale_recv.at[source],
            device_id={"tp": tp, "seq": source},
            device_id_type=MESH,
        ).wait_recv()
    factor = scales[...].reshape(n_seq * picks, HEAD_DIM)[:, :1]

    for j in range(cols // tile):
        total = part[j, tp].astype(jnp.float32)
        for step in range(1, n_tp):
            source = (tp + step) % n_tp
            pltpu.make_async_remote_copy(
                src_ref=part.at[j, 0],
                dst_ref=red.at[j, source],
                send_sem=red_send.at[step, j],
                recv_sem=red_recv.at[source, j],
                device_id={"tp": source, "seq": seq},
                device_id_type=MESH,
            ).wait_recv()
            total = total + red[j, source].astype(jnp.float32)
        sum_ref[:, j * tile : (j + 1) * tile] = (total * factor).astype(jnp.bfloat16)

    for j in range(cols // tile):
        for step in range(1, n_tp):
            reduce(step, j).wait_send()
    for step in range(1, n_seq):
        scale_to(step).wait_send()


def on_device(n_tp, n_seq, queries, keys, values, mem_pos, norm_gain, summary_weight):
    rows = queries.shape[0]
    picks = mem_pos.shape[0]
    prior = -(-(WINDOW - 1) // rows)
    n = n_tp * n_seq
    width = summary_weight.shape[0]
    cols = summary_weight.shape[1]
    per = KV_HEADS // n_tp
    chunks = KV_HEADS // per
    columns = width // per
    tiles = cols // 512 if cols % 512 == 0 else 1
    vmem = pl.BlockSpec(memory_space=pltpu.VMEM)
    anywhere = pl.BlockSpec(memory_space=pl.ANY)
    bf16 = jnp.bfloat16
    dma = pltpu.SemaphoreType.DMA
    span = (prior + 1) * rows
    results = pl.pallas_call(
        functools.partial(kernel, n_tp, n_seq, prior),
        out_shape=(
            jax.ShapeDtypeStruct((rows, D), bf16),
            jax.ShapeDtypeStruct((n_seq * picks, cols), bf16),
        ),
        in_specs=[
            anywhere, vmem, vmem, pl.BlockSpec(memory_space=pltpu.SMEM), vmem, anywhere,
        ],
        out_specs=(anywhere, vmem),
        scratch_shapes=[
            pltpu.VMEM((rows, D), bf16),
            pltpu.VMEM((width, cols), bf16),
            pltpu.VMEM((KV_HEADS, 2, span, HEAD_DIM), bf16),
            pltpu.VMEM((span, rows), jnp.float32),
            pltpu.VMEM((picks, HEAD_DIM), jnp.float32),
            pltpu.VMEM((chunks, per * picks, columns), bf16),
            pltpu.VMEM((n, per * picks, columns), bf16),
            pltpu.VMEM((tiles, n_tp, n_seq * picks, cols // tiles), bf16),
            pltpu.VMEM((tiles, n_tp, n_seq * picks, cols // tiles), bf16),
            pltpu.VMEM((n_seq, picks, HEAD_DIM), jnp.float32),
            pltpu.VMEM((rows, D), bf16),
            dma((chunks,)),
            dma((2,)),
            dma((prior + 1, chunks)),
            dma((prior + 1, chunks)),
            dma((chunks, n_seq)),
            dma((n,)),
            dma((n_tp, tiles)),
            dma((n_tp, tiles)),
            dma((n_seq,)),
            dma((n_seq,)),
        ],
        compiler_params=pltpu.CompilerParams(
            collective_id=0, has_side_effects=True, vmem_limit_bytes=60 * 1024 * 1024
        ),
        cost_estimate=pl.CostEstimate(
            flops=4 * HEADS * rows * span * HEAD_DIM + 2 * n * picks * width * cols,
            bytes_accessed=2 * (2 * rows * D + 4 * rows * KV_HEADS * HEAD_DIM + width * cols),
            transcendentals=HEADS * rows * span,
        ),
    )(queries, keys, values, mem_pos, norm_gain.reshape(1, D), summary_weight)
    return pl.pallas_call(
        hand_over,
        out_shape=tuple(jax.ShapeDtypeStruct(r.shape, r.dtype) for r in results),
        in_specs=[anywhere, anywhere],
        out_specs=(anywhere, anywhere),
        scratch_shapes=[
            *(pltpu.VMEM(r.shape, r.dtype) for r in results),
            dma((2, PIECES + 1)),
        ],
        compiler_params=pltpu.CompilerParams(vmem_limit_bytes=60 * 1024 * 1024),
    )(*results)


def solution(mesh):
    placed = (
        P(("file", "tp", "seq"), None),
        P(("file", "tp", "seq"), None),
        P(("file", "tp", "seq"), None),
        P(("file", "tp", "seq")),
        P(),
        P("tp", "seq"),
    )
    return jax.shard_map(
        functools.partial(on_device, mesh.shape["tp"], mesh.shape["seq"]),
        mesh=mesh,
        in_specs=placed,
        out_specs=(P(("file", "tp", "seq"), None), P(("file", "tp"), "seq")),
        check_vma=False,
    )
```

```python
import functools
import math

import jax
import jax.numpy as jnp
from jax import lax
from jax.experimental import pallas as pl
from jax.experimental.pallas import tpu as pltpu
from jax.sharding import PartitionSpec as P

D = 4096
HEADS = 32
KV_HEADS = 8
HEAD_DIM = 128
WINDOW = 512
SHARE = HEADS // KV_HEADS
MESH = pl.DeviceIdType.MESH
AHEAD = 2
LEAD = 1
LAG = 1
PIECES = 4


def hand_over(enc_from, sum_from, enc_to, sum_to, enc_buf, sum_buf, sems):
    rows = enc_from.shape[0] // PIECES
    parts = [(sum_from, sum_buf, sum_to)]
    for i in range(PIECES):
        piece = pl.ds(i * rows, rows)
        parts.append((enc_from.at[piece], enc_buf.at[piece], enc_to.at[piece]))
    into = [pltpu.make_async_copy(a, b, sems.at[0, i]) for i, (a, b, c) in enumerate(parts)]
    out = [pltpu.make_async_copy(b, c, sems.at[1, i]) for i, (a, b, c) in enumerate(parts)]
    for copy in into:
        copy.start()
    for first, second in zip(into, out):
        first.wait()
        second.start()
    for copy in out:
        copy.wait()


def kernel(
    n_tp, n_seq, prior,
    q_hbm, k_hbm, v_hbm, pos_ref, gain_ref, w_hbm,
    enc_ref, sum_ref,
    q_buf, k_ref, v_ref, w_buf, kv, bias, squares, mine, mem, part, red, scales, enc_buf, enc_sem,
    local_sem, kv_send, kv_recv, mem_send, mem_recv, red_send, red_recv, scale_send, scale_recv,
):
    tp = lax.axis_index("tp")
    seq = lax.axis_index("seq")
    me = tp * n_seq + seq
    n = n_tp * n_seq
    rows = k_ref.shape[0]
    assert rows == HEAD_DIM
    span = (prior + 1) * rows
    picks = pos_ref.shape[0]
    per = KV_HEADS // n_tp
    columns = SHARE * HEAD_DIM
    chunks = KV_HEADS // per
    cols = sum_ref.shape[1]
    tile = 512 if cols % 512 == 0 else cols
    squares[...] = jnp.zeros_like(squares)

    def device(index):
        return {"tp": index // n_seq, "seq": index % n_seq}

    barrier = pltpu.get_barrier_semaphore()

    @pl.loop(1, n)
    def _(step):
        pl.semaphore_signal(
            barrier, inc=1, device_id=device((me + step) % n), device_id_type=MESH
        )

    k_copy = pltpu.make_async_copy(k_hbm, k_ref, local_sem.at[2])
    v_copy = pltpu.make_async_copy(v_hbm, v_ref, local_sem.at[3])
    q_copy = pltpu.make_async_copy(q_hbm, q_buf, local_sem.at[0])
    w_copy = pltpu.make_async_copy(w_hbm, w_buf, local_sem.at[1])
    for copy in (k_copy, v_copy, q_copy, w_copy):
        copy.start()
    k_copy.wait()
    v_copy.wait()
    for g in range(KV_HEADS):
        kv[g, 0, prior * rows :, :] = k_ref[:, g * HEAD_DIM : (g + 1) * HEAD_DIM]
        kv[g, 1, prior * rows :, :] = v_ref[:, g * HEAD_DIM : (g + 1) * HEAD_DIM].T
    for k in range(1, prior + 1):

        @pl.when(me < k)
        def _():
            start = (prior - k) * rows
            kv[:, :, start : start + rows, :] = jnp.zeros(
                (KV_HEADS, 2, rows, HEAD_DIM), jnp.bfloat16
            )

    row = lax.broadcasted_iota(jnp.int32, (span, rows), 1)
    col = lax.broadcasted_iota(jnp.int32, (span, rows), 0) - prior * rows
    seen = (col <= row) & (col > row - WINDOW) & (col + me * rows >= 0)
    bias[...] = jnp.where(seen, 0.0, -jnp.inf).astype(jnp.float32)

    pick_row = lax.broadcasted_iota(jnp.int32, (picks, rows), 0)
    pick_col = lax.broadcasted_iota(jnp.int32, (picks, rows), 1)
    wanted = jnp.zeros((picks, rows), jnp.int32)
    for j in range(picks):
        wanted = jnp.where(pick_row == j, pos_ref[j] - me * rows, wanted)
    choose = jnp.where(pick_col == wanted, 1.0, 0.0).astype(jnp.bfloat16)

    def slot(c, k):
        return kv.at[pl.ds(c * per, per), :, pl.ds((prior - k) * rows, rows), :]

    def send(c, k, lands, target, way):
        return pltpu.make_async_remote_copy(
            src_ref=slot(c, k),
            dst_ref=slot(c, lands),
            send_sem=kv_send.at[way, c],
            recv_sem=kv_recv.at[lands, c],
            device_id=target,
            device_id_type=MESH,
        )

    def each_own(c, act):
        for k in range(1, prior + 1):
            direct = me + k < n
            if k == 1:
                direct = direct & (seq + 1 < n_seq)
            if k == 3:
                direct = direct & (seq + 3 >= n_seq)

            @pl.when(direct)
            def _():
                act(send(c, 0, k, device(me + k), k))

    def each_forward(c, act):
        @pl.when((seq >= 2) & (seq + 1 < n_seq))
        def _():
            act(send(c, 2, 3, device(me + 1), 0))

        @pl.when((seq == 1) & (tp > 0))
        def _():
            act(send(c, 2, 1, device(me - 1), 0))

    def arrive(c, k):
        @pl.when(me >= k)
        def _():
            send(c, 0, k, device(me), k).wait_recv()

    def own(c):
        each_own(c, lambda copy: copy.start())

    def forward(c):
        arrive(c, 2)
        each_forward(c, lambda copy: copy.start())

    fold = math.log2(math.e) / HEAD_DIM**0.5

    def attend(q_all, keys, flipped, bias):
        q_rows = jnp.concatenate(
            [q_all[:, h * HEAD_DIM : (h + 1) * HEAD_DIM] for h in range(SHARE)], axis=0
        )
        scores = lax.dot_general(
            keys, q_rows, (((1,), (1,)), ((), ())), preferred_element_type=jnp.float32
        )
        masked = scores + jnp.concatenate([bias[...]] * SHARE, axis=1)
        peak = jnp.max(masked, axis=0, keepdims=True)
        weights = jnp.exp2((masked - peak) * fold)
        total = jnp.sum(weights, axis=0, keepdims=True)
        values = jnp.concatenate(
            [flipped[b * rows : (b + 1) * rows] for b in range(prior + 1)], axis=1
        )
        mixed = jnp.dot(values, weights.astype(jnp.bfloat16), preferred_element_type=jnp.float32)
        mixed = mixed * (1.0 / total)
        return jnp.concatenate(
            [mixed[:, h * rows : (h + 1) * rows].T for h in range(SHARE)], axis=1
        ).astype(jnp.bfloat16)

    def encode(c):
        gained = []
        for j in range(per):
            g = c * per + j
            first = pl.multiple_of(g * columns, columns)
            encoded = attend(q_buf[:, pl.ds(first, columns)], kv[g, 0], kv[g, 1], bias)
            enc_buf[:, pl.ds(first, columns)] = encoded
            picked = jnp.dot(choose, encoded, preferred_element_type=jnp.float32)
            squared = picked * picked
            for h in range(SHARE):
                squares[...] += squared[:, h * HEAD_DIM : (h + 1) * HEAD_DIM]
            gained.append(picked * gain_ref[:, pl.ds(first, columns)])
        mine[c] = jnp.concatenate(gained, axis=0).astype(jnp.bfloat16)

    def write(c):
        where = pl.ds(pl.multiple_of(c * per * columns, columns), per * columns)
        return pltpu.make_async_copy(enc_buf.at[:, where], enc_ref.at[:, where], enc_sem.at[c])

    def share(c, s, source):
        return pltpu.make_async_remote_copy(
            src_ref=mine.at[c],
            dst_ref=mem.at[source],
            send_sem=mem_send.at[c, s],
            recv_sem=mem_recv.at[source],
            device_id={"tp": c, "seq": s},
            device_id_type=MESH,
        )

    def each_share(c, act):
        for step in range(1, n_seq):
            act(share(c, (seq + step) % n_seq, me))

        @pl.when(c != tp)
        def _():
            act(share(c, seq, me))

    def scale_to(step):
        return pltpu.make_async_remote_copy(
            src_ref=scales.at[seq],
            dst_ref=scales.at[seq],
            send_sem=scale_send.at[step],
            recv_sem=scale_recv.at[seq],
            device_id={"tp": tp, "seq": (seq + step) % n_seq},
            device_id_type=MESH,
        )

    def reduce(step, j):
        other = (tp + step) % n_tp
        return pltpu.make_async_remote_copy(
            src_ref=part.at[j, other],
            dst_ref=red.at[j, tp],
            send_sem=red_send.at[step, j],
            recv_sem=red_recv.at[tp, j],
            device_id={"tp": other, "seq": seq},
            device_id_type=MESH,
        )

    def project():
        @pl.loop(1, n)
        def _(step):
            source = (me + step) % n
            share(tp, seq, source).wait_recv()

        gathered = mem[...].astype(jnp.float32)
        memory = jnp.concatenate(
            [
                gathered[:, j * picks : (j + 1) * picks].reshape(n * picks, columns)
                for j in range(per)
            ],
            axis=1,
        ).astype(jnp.bfloat16)
        for j in range(cols // tile):
            where = slice(j * tile, (j + 1) * tile)
            sums = jnp.dot(memory, w_buf[:, where], preferred_element_type=jnp.float32)
            part[j] = sums.reshape(n_tp, n_seq * picks, tile).astype(jnp.bfloat16)
            for step in range(1, n_tp):
                reduce(step, j).start()

    pl.semaphore_wait(barrier, n - 1)
    for c in range(AHEAD):
        own(c)
    for c in range(LEAD):
        forward(c)
    q_copy.wait()
    w_copy.wait()

    @pl.loop(0, chunks + LAG)
    def _(g):
        @pl.when(g + AHEAD < chunks)
        def _():
            own(g + AHEAD)

        @pl.when(g + LEAD < chunks)
        def _():
            forward(g + LEAD)

        @pl.when(g < chunks)
        def _():
            for k in range(1, prior + 1):
                if k != 2:
                    arrive(g, k)
            encode(g)
            each_share(g, lambda copy: copy.start())
            write(g).start()

            @pl.when(g == tp)
            def _():
                mem[me] = mine[g]

        @pl.when(g == chunks - 1)
        def _():
            meansq = jnp.sum(squares[...], axis=1, keepdims=True) / D
            scales[seq] = jnp.broadcast_to(lax.rsqrt(meansq + 1e-05), scales.shape[1:])
            for step in range(1, n_seq):
                scale_to(step).start()

        @pl.when(g - LAG == tp)
        def _():
            project()

    @pl.loop(0, chunks)
    def _(c):
        write(c).wait()
        each_share(c, lambda copy: copy.wait_send())
        each_own(c, lambda copy: copy.wait_send())
        each_forward(c, lambda copy: copy.wait_send())

    for step in range(1, n_seq):
        source = (seq + step) % n_seq
        pltpu.make_async_remote_copy(
            src_ref=scales.at[source],
            dst_ref=scales.at[source],
            send_sem=scale_send.at[step],
            recv_sem=scale_recv.at[source],
            device_id={"tp": tp, "seq": source},
            device_id_type=MESH,
        ).wait_recv()
    factor = scales[...].reshape(n_seq * picks, HEAD_DIM)[:, :1]

    for j in range(cols // tile):
        total = part[j, tp].astype(jnp.float32)
        for step in range(1, n_tp):
            source = (tp + step) % n_tp
            pltpu.make_async_remote_copy(
                src_ref=part.at[j, 0],
                dst_ref=red.at[j, source],
                send_sem=red_send.at[step, j],
                recv_sem=red_recv.at[source, j],
                device_id={"tp": source, "seq": seq},
                device_id_type=MESH,
            ).wait_recv()
            total = total + red[j, source].astype(jnp.float32)
        sum_ref[:, j * tile : (j + 1) * tile] = (total * factor).astype(jnp.bfloat16)

    for j in range(cols // tile):
        for step in range(1, n_tp):
            reduce(step, j).wait_send()
    for step in range(1, n_seq):
        scale_to(step).wait_send()


def on_device(n_tp, n_seq, queries, keys, values, mem_pos, norm_gain, summary_weight):
    rows = queries.shape[0]
    picks = mem_pos.shape[0]
    prior = -(-(WINDOW - 1) // rows)
    n = n_tp * n_seq
    width = summary_weight.shape[0]
    cols = summary_weight.shape[1]
    per = KV_HEADS // n_tp
    chunks = KV_HEADS // per
    columns = width // per
    tiles = cols // 512 if cols % 512 == 0 else 1
    vmem = pl.BlockSpec(memory_space=pltpu.VMEM)
    anywhere = pl.BlockSpec(memory_space=pl.ANY)
    bf16 = jnp.bfloat16
    dma = pltpu.SemaphoreType.DMA
    span = (prior + 1) * rows
    results = pl.pallas_call(
        functools.partial(kernel, n_tp, n_seq, prior),
        out_shape=(
            jax.ShapeDtypeStruct((rows, D), bf16),
            jax.ShapeDtypeStruct((n_seq * picks, cols), bf16),
        ),
        in_specs=[
            anywhere, anywhere, anywhere, pl.BlockSpec(memory_space=pltpu.SMEM), vmem, anywhere,
        ],
        out_specs=(anywhere, vmem),
        scratch_shapes=[
            pltpu.VMEM((rows, D), bf16),
            pltpu.VMEM(keys.shape, bf16),
            pltpu.VMEM(values.shape, bf16),
            pltpu.VMEM((width, cols), bf16),
            pltpu.VMEM((KV_HEADS, 2, span, HEAD_DIM), bf16),
            pltpu.VMEM((span, rows), jnp.float32),
            pltpu.VMEM((picks, HEAD_DIM), jnp.float32),
            pltpu.VMEM((chunks, per * picks, columns), bf16),
            pltpu.VMEM((n, per * picks, columns), bf16),
            pltpu.VMEM((tiles, n_tp, n_seq * picks, cols // tiles), bf16),
            pltpu.VMEM((tiles, n_tp, n_seq * picks, cols // tiles), bf16),
            pltpu.VMEM((n_seq, picks, HEAD_DIM), jnp.float32),
            pltpu.VMEM((rows, D), bf16),
            dma((chunks,)),
            dma((4,)),
            dma((prior + 1, chunks)),
            dma((prior + 1, chunks)),
            dma((chunks, n_seq)),
            dma((n,)),
            dma((n_tp, tiles)),
            dma((n_tp, tiles)),
            dma((n_seq,)),
            dma((n_seq,)),
        ],
        compiler_params=pltpu.CompilerParams(
            collective_id=0, has_side_effects=True, vmem_limit_bytes=60 * 1024 * 1024
        ),
        cost_estimate=pl.CostEstimate(
            flops=4 * HEADS * rows * span * HEAD_DIM + 2 * n * picks * width * cols,
            bytes_accessed=2 * (2 * rows * D + 4 * rows * KV_HEADS * HEAD_DIM + width * cols),
            transcendentals=HEADS * rows * span,
        ),
    )(queries, keys, values, mem_pos, norm_gain.reshape(1, D), summary_weight)
    return pl.pallas_call(
        hand_over,
        out_shape=tuple(jax.ShapeDtypeStruct(r.shape, r.dtype) for r in results),
        in_specs=[anywhere, anywhere],
        out_specs=(anywhere, anywhere),
        scratch_shapes=[
            *(pltpu.VMEM(r.shape, r.dtype) for r in results),
            dma((2, PIECES + 1)),
        ],
        compiler_params=pltpu.CompilerParams(vmem_limit_bytes=60 * 1024 * 1024),
    )(*results)


def solution(mesh):
    placed = (
        P(("file", "tp", "seq"), None),
        P(("file", "tp", "seq"), None),
        P(("file", "tp", "seq"), None),
        P(("file", "tp", "seq")),
        P(),
        P("tp", "seq"),
    )
    return jax.shard_map(
        functools.partial(on_device, mesh.shape["tp"], mesh.shape["seq"]),
        mesh=mesh,
        in_specs=placed,
        out_specs=(P(("file", "tp", "seq"), None), P(("file", "tp"), "seq")),
        check_vma=False,
    )
```
